256 devices in a mesh: seq: 32 (over x, y, core), head: 8 (over z).
Axes of the slice: x: 4, y: 4, z: 8, core: 2. Of those that a mesh axis runs over, the one named last changes fastest.
Arguments:
- key_rows: bfloat16 [8192, 2048], P('seq', 'head'), may hold values from -1 to 1, as said below
- values: bfloat16 [8192, 2048], P('seq', 'head'), may hold values from -6 to 6
- d_layer: bfloat16 [8192, 2048], P('seq', 'head'), may hold values from -6 to 6
- out_weight: bfloat16 [2048, 2048], P('head'), may hold values from -0.125 to 0.125
- saved_solutions: float32 [8192, 2048], P('seq', 'head'), may hold values from -0.3125 to 0.3125
- ridge_scale: float32 [16], P('head'), may hold values from 0.5 to 4
Outputs:
- grad_queries: float32 [8192, 2048], P('seq', 'head')
- grad_keys: float32 [8192, 2048], P('seq', 'head')
- grad_values: float32 [8192, 2048], P('seq', 'head')
The draws below stay inside these ranges and needn't reach their ends.
Inputs may be any that keep to these rules, and one draw needn't show every extreme that they name: `key_rows`: within each head the 128 entries of a key have Euclidean norm 1 up to bfloat16 rounding.
All inputs are finite; a program needn't handle non-finite values.
Results may differ from the reference program's by a relative error of at most 0.0029.
Values may be sent and summed in bfloat16 or wider, within the bound.
No kernel may reach another device: no remote copies, remote signals or barrier semaphores. Data moves between devices by JAX's collectives and lax.ppermute only.
A program may use at most 64 MiB of HBM per device.

```python
import math
import jax
import jax.numpy as jnp
from jax import lax

DM = 2048
HEADS = 16
DH = 128
TOK_DEV = 256
ITERS = 8
WIN = 2048
TOKENS = 8192


def draw_key_rows(key, part):
    scale_key = jax.random.fold_in(key, 11)
    entry_key = jax.random.fold_in(key, 23)
    channel_scales = jnp.exp(jax.random.uniform(scale_key, (HEADS * DH,), jnp.float32, jnp.log(0.3), jnp.log(1.5)))
    entries = jnp.clip(jax.random.normal(entry_key, (TOKENS, HEADS * DH), jnp.float32), -6.0, 6.0)
    scaled = (entries * channel_scales).reshape(TOKENS, HEADS, DH)
    lengths = jnp.sqrt(jnp.sum(scaled * scaled, axis=-1, keepdims=True) + 1e-06)
    return (scaled / lengths).reshape(TOKENS, HEADS * DH).astype(jnp.bfloat16)


def levels(stream_key, extent, cuts, least, largest):
    level, own = 1.0, jax.random.fold_in(stream_key, 6)
    for axis_at, parts in cuts:
        steps = jnp.exp(jax.random.uniform(jax.random.fold_in(own, axis_at), (parts,), jnp.float32, least / len(cuts), largest / len(cuts)))
        level = level * jnp.repeat(steps, extent[axis_at] // parts).reshape([-1 if axis == axis_at else 1 for axis in range(len(extent))])
    return level


def normal_values(stream_key, extent, spread, bound, pieces=(), kind=jnp.bfloat16):
    factor_of = levels(stream_key, extent, pieces, -0.22, 0.18) if pieces else 1.0
    values = jax.random.normal(stream_key, extent, jnp.float32) * spread * factor_of
    return jnp.minimum(jnp.maximum(values, -bound), bound).astype(kind)


def setup_inputs(seed: int = 0) -> dict:
    arg_keys = jax.random.split(jax.random.key(seed), 7)
    key_rows = draw_key_rows(jax.random.fold_in(arg_keys[6], 71), 0)
    values = normal_values(arg_keys[1], (TOKENS, HEADS * DH), 1.0, 6.0, ((0, 32), (1, 8)))
    d_layer = normal_values(arg_keys[2], (TOKENS, DM), 1.0, 6.0, ((0, 32), (1, 8)))
    out_weight = normal_values(arg_keys[3], (HEADS * DH, DM), DM ** -0.5, 0.125, ((0, 8),))
    saved_solutions = normal_values(arg_keys[4], (TOKENS, HEADS * DH), (WIN ** -0.5), 0.3125, ((0, 32), (1, 8)), jnp.float32)
    ridge_scale = jnp.clip(jnp.exp(math.log(4.0) - 2.0794415 * jax.random.uniform(arg_keys[5], (HEADS,), jnp.float32) ** levels(arg_keys[5], (HEADS,), ((0, 8),), -0.2, 0.2)), 0.5, 4.0)
    return dict(key_rows=key_rows, values=values, d_layer=d_layer, out_weight=out_weight, saved_solutions=saved_solutions, ridge_scale=ridge_scale)


HIGHEST_PRECISION = lax.Precision.HIGHEST
EPSILON = 1e-6


def make_lower(block_len):
    row_ids = lax.broadcasted_iota(jnp.int32, (block_len, block_len), 0)
    col_ids = lax.broadcasted_iota(jnp.int32, (block_len, block_len), 1)
    return (row_ids >= col_ids).astype(jnp.float32)


def shift_down(blocks, amount):
    padding = jnp.zeros((amount,) + blocks.shape[1:], blocks.dtype)
    return jnp.concatenate([padding, blocks[: blocks.shape[0] - amount]], axis=0)


def shift_up(blocks, amount):
    padding = jnp.zeros((amount,) + blocks.shape[1:], blocks.dtype)
    return jnp.concatenate([blocks[amount:], padding], axis=0)


def masked_apply(left, right, carried, mask_table):
    scores = jnp.einsum("bid,bjd->bij", left, right, precision=HIGHEST_PRECISION) * mask_table
    return jnp.einsum("bij,bjd->bid", scores, carried, precision=HIGHEST_PRECISION)


def outer_sums(left, right):
    return jnp.einsum("bid,bie->bde", left, right, precision=HIGHEST_PRECISION)


def one_head(operands):
    key_part, value_part, saved_part, dout_part, ridge_value = operands
    block_len = min(512, TOK_DEV)
    block_count = TOKENS // block_len
    lag_blocks = WIN // block_len
    key_blk = key_part.reshape(block_count, block_len, DH)
    val_blk = value_part.reshape(block_count, block_len, DH)
    sav_blk = saved_part.reshape(block_count, block_len, DH)
    out_blk = dout_part.reshape(block_count, block_len, DH)
    lower_table = make_lower(block_len)
    upper_table = lower_table.T

    gram_blocks = outer_sums(key_blk, key_blk)
    state_blocks = outer_sums(val_blk, key_blk)
    gram_before = jnp.cumsum(gram_blocks, axis=0) - gram_blocks
    state_before = jnp.cumsum(state_blocks, axis=0) - state_blocks
    gram_base = gram_before - shift_down(gram_before, lag_blocks)
    state_base = state_before - shift_down(state_before, lag_blocks)
    key_lag = shift_down(key_blk, lag_blocks)
    val_lag = shift_down(val_blk, lag_blocks)

    adjoint_rhs = jnp.einsum("bif,bfe->bie", out_blk, state_base, precision=HIGHEST_PRECISION)
    adjoint_rhs = adjoint_rhs + masked_apply(out_blk, val_blk, key_blk, lower_table)
    adjoint_rhs = adjoint_rhs - masked_apply(out_blk, val_lag, key_lag, lower_table)

    def apply_gram(vectors):
        result = jnp.einsum("bid,bde->bie", vectors, gram_base, precision=HIGHEST_PRECISION)
        result = result + masked_apply(vectors, key_blk, key_blk, lower_table)
        result = result - masked_apply(vectors, key_lag, key_lag, lower_table)
        return result + ridge_value * vectors

    solution = jnp.zeros_like(adjoint_rhs)
    residual_now = adjoint_rhs
    direction = adjoint_rhs
    norm_now = jnp.sum(residual_now * residual_now, axis=-1, keepdims=True)
    for iteration in range(ITERS):
        image = apply_gram(direction)
        alpha = norm_now / (jnp.sum(direction * image, axis=-1, keepdims=True) + EPSILON)
        solution = solution + alpha * direction
        residual_now = residual_now - alpha * image
        norm_next = jnp.sum(residual_now * residual_now, axis=-1, keepdims=True)
        direction = residual_now + (norm_next / (norm_now + EPSILON)) * direction
        norm_now = norm_next

    pair_blocks = outer_sums(solution, sav_blk)
    cross_blocks = outer_sums(sav_blk, out_blk)
    pair_after = jnp.flip(jnp.cumsum(jnp.flip(pair_blocks, 0), axis=0), 0) - pair_blocks
    cross_after = jnp.flip(jnp.cumsum(jnp.flip(cross_blocks, 0), axis=0), 0) - cross_blocks
    pair_base = pair_after - shift_up(pair_after, lag_blocks)
    cross_base = cross_after - shift_up(cross_after, lag_blocks)
    sym_base = pair_base + jnp.swapaxes(pair_base, 1, 2)

    sol_lead = shift_up(solution, lag_blocks)
    sav_lead = shift_up(sav_blk, lag_blocks)
    out_lead = shift_up(out_blk, lag_blocks)

    grad_k = -jnp.einsum("bid,bde->bie", key_blk, sym_base, precision=HIGHEST_PRECISION)
    grad_k = grad_k + jnp.einsum("bif,bef->bie", val_blk, cross_base, precision=HIGHEST_PRECISION)
    grad_k = grad_k - masked_apply(key_blk, sav_blk, solution, upper_table)
    grad_k = grad_k - masked_apply(key_blk, solution, sav_blk, upper_table)
    grad_k = grad_k + masked_apply(val_blk, out_blk, sav_blk, upper_table)
    grad_k = grad_k + masked_apply(key_blk, sav_lead, sol_lead, upper_table)
    grad_k = grad_k + masked_apply(key_blk, sol_lead, sav_lead, upper_table)
    grad_k = grad_k - masked_apply(val_blk, out_lead, sav_lead, upper_table)

    grad_v = jnp.einsum("bid,bdf->bif", key_blk, cross_base, precision=HIGHEST_PRECISION)
    grad_v = grad_v + masked_apply(key_blk, sav_blk, out_blk, upper_table)
    grad_v = grad_v - masked_apply(key_blk, sav_lead, out_lead, upper_table)

    return (solution.reshape(TOKENS, DH), grad_k.reshape(TOKENS, DH), grad_v.reshape(TOKENS, DH))


def reference(key_rows, values, d_layer, out_weight, saved_solutions, ridge_scale):
    d_heads = jnp.dot(d_layer, out_weight.T, preferred_element_type=jnp.float32).astype(jnp.bfloat16)

    def by_head(array):
        return array.astype(jnp.float32).reshape(TOKENS, HEADS, DH).transpose(1, 0, 2)

    grads = lax.map(one_head, (by_head(key_rows), by_head(values), by_head(saved_solutions),
                               by_head(d_heads), ridge_scale.astype(jnp.float32)))

    def by_token(array):
        return array.transpose(1, 0, 2).reshape(TOKENS, HEADS * DH).astype(jnp.float32)

    return by_token(grads[0]), by_token(grads[1]), by_token(grads[2])
```

```python
import jax
import jax.numpy as jnp
from jax import lax
from jax.experimental import pallas as pl
from jax.experimental.pallas import tpu as pltpu
from jax.sharding import PartitionSpec as P

DH = 128
TOK = 256
NH = 2
ITERS = 8
EPSILON = 1e-06
F32 = jnp.float32
BF16 = jnp.bfloat16
VM = pl.BlockSpec(memory_space=pltpu.VMEM)
SM = pl.BlockSpec(memory_space=pltpu.SMEM)
PARAMS = pltpu.CompilerParams(vmem_limit_bytes=24 * 1024 * 1024)


def mm(a, b):
    return lax.dot_general(a, b, (((1,), (0,)), ((), ())), preferred_element_type=F32)


def mm_nt(a, b):
    return lax.dot_general(a, b, (((1,), (1,)), ((), ())), preferred_element_type=F32)


def mm_tn(a, b):
    return lax.dot_general(a, b, (((0,), (0,)), ((), ())), preferred_element_type=F32)


def split(a):
    hi = a.astype(BF16)
    return hi, (a - hi.astype(F32)).astype(BF16)


def head(ref, h, base=0):
    return ref[:, base + h * DH : base + (h + 1) * DH]


def tri(rows, cols):
    r = lax.broadcasted_iota(jnp.int32, (rows, cols), 0)
    c = lax.broadcasted_iota(jnp.int32, (rows, cols), 1)
    return r, c


def call(kernel, outs, *args, flops=0, smem=()):
    return pl.pallas_call(
        kernel,
        out_shape=[jax.ShapeDtypeStruct(s, d) for s, d in outs],
        in_specs=[SM if i in smem else VM for i in range(len(args))],
        out_specs=[VM] * len(outs),
        compiler_params=PARAMS,
        cost_estimate=pl.CostEstimate(flops=flops, bytes_accessed=1 << 19, transcendentals=0),
    )(*args)


def own_states(k_ref, v_ref, x_ref, t_ref, kv_ref, xb_ref):
    for h in range(NH):
        k = head(k_ref, h)
        t_ref[h] = mm_tn(k, k)
        t_ref[NH + h] = mm_tn(head(v_ref, h), k)
    kv_ref[:, : NH * DH] = k_ref[...]
    kv_ref[:, NH * DH :] = v_ref[...]
    xb_ref[...] = x_ref[...].astype(BF16)


def states_to_send(t_ref, lag_ref, p1_ref, p2_ref, part_ref, send_ref):
    core = lax.rem(lax.axis_index("seq"), 2)
    for h in range(NH):
        k = head(lag_ref, h)
        lag_g = mm_tn(k, k)
        lag_s = mm_tn(head(lag_ref, h, NH * DH), k)
        for at, lag in ((h, lag_g), (NH + h, lag_s)):
            part = p1_ref[at] + p2_ref[at]
            part_ref[at] = part
            send_ref[at] = part + jnp.where(core == 0, t_ref[at], lag)


def adjoints(d_ref, w_ref, kv_ref, lag_ref, x_ref, part_ref, recv_ref, ridge_ref, y_ref, yo_ref, t_ref):
    B = 128
    out = mm_nt(d_ref[0], w_ref[:, :256])
    for z in range(1, 8):
        out = out + mm_nt(d_ref[z], w_ref[:, z * 256 : (z + 1) * 256])
    out = out.astype(BF16)
    yo_ref[:, 256:] = out
    rows, cols = tri(B, B)
    low, up = rows >= cols, rows < cols

    rhs, keys, ps, ridges = [], [], [], []
    for h in range(NH):
        k, v = head(kv_ref, h), head(kv_ref, h, 256)
        kl, vl = head(lag_ref, h), head(lag_ref, h, 256)
        gram = part_ref[h] + recv_ref[h]
        state = part_ref[NH + h] + recv_ref[NH + h]
        o = out[:, h * DH : (h + 1) * DH]
        for b in range(2):
            kb, vb = k[b * B : (b + 1) * B], v[b * B : (b + 1) * B]
            klb, vlb = kl[b * B : (b + 1) * B], vl[b * B : (b + 1) * B]
            ob = o[b * B : (b + 1) * B]
            kf, vf = (kl[B:], vl[B:]) if b == 0 else (k[:B], v[:B])
            g = gram + mm_tn(kf, kf)
            s = state + mm_tn(vf, kf)
            g_hi, g_lo = split(g)
            kbt = kb.astype(F32).T.astype(BF16)
            klbt = klb.astype(F32).T.astype(BF16)
            half = jnp.concatenate([g_hi, kbt, klbt, g_lo], axis=1)
            rhs.append(jnp.concatenate([half, half], axis=0))
            both = jnp.concatenate([kb, klb], axis=0)
            keys.append(jnp.concatenate([both, both], axis=0))
            sc = jnp.concatenate(
                [jnp.where(low, mm_nt(ob, vb), 0.0), jnp.where(up, mm_nt(ob, vlb), 0.0)], axis=1
            )
            sc_hi, sc_lo = split(sc)
            s_hi, s_lo = split(s)
            p = mm(ob, s_hi) + mm(ob, s_lo)
            p = p + mm(jnp.concatenate([sc_hi, sc_lo], axis=1), keys[-1])
            ps.append(p)
            ridges.append(ridge_ref[h])

    n = len(ps)

    def apply_gram(p, i):
        p_hi, p_lo = split(p)
        r = mm(jnp.concatenate([p_hi, p_lo], axis=1), rhs[i])
        sc = jnp.concatenate(
            [jnp.where(low, r[:, B : 2 * B], 0.0), jnp.where(up, r[:, 2 * B : 3 * B], 0.0)], axis=1
        )
        sc_hi, sc_lo = split(sc)
        t = mm(jnp.concatenate([sc_hi, sc_lo], axis=1), keys[i])
        return t + r[:, :B] + r[:, 3 * B :] + ridges[i] * p

    ys = [jnp.zeros((B, DH), F32)] * n
    rs = list(ps)
    rrs = [jnp.sum(r * r, axis=-1, keepdims=True) for r in rs]
    for it in range(ITERS):
        for i in range(n):
            a = apply_gram(ps[i], i)
            alpha = rrs[i] / (jnp.sum(ps[i] * a, axis=-1, keepdims=True) + EPSILON)
            ys[i] = ys[i] + alpha * ps[i]
            if it < ITERS - 1:
                rs[i] = rs[i] - alpha * a
                nr = jnp.sum(rs[i] * rs[i], axis=-1, keepdims=True)
                ps[i] = rs[i] + nr / (rrs[i] + EPSILON) * ps[i]
                rrs[i] = nr

    for h in range(NH):
        y = jnp.concatenate([ys[2 * h], ys[2 * h + 1]], axis=0)
        y_ref[:, h * DH : (h + 1) * DH] = y
        yo_ref[:, h * DH : (h + 1) * DH] = y.astype(BF16)
        y_hi, y_lo = split(y)
        x_hi, x_lo = split(head(x_ref, h))
        o = out[:, h * DH : (h + 1) * DH]
        pair = mm_tn(y_hi, x_hi) + mm_tn(y_lo, x_hi) + mm_tn(y_hi, x_lo)
        t_ref[h] = pair + pair.T
        t_ref[NH + h] = mm_tn(x_hi, o) + mm_tn(x_lo, o)


def near_terms(kv_ref, xb_ref, yo_ref, xl_ref, yol_ref, t_ref, gk_ref, gv_ref, extra_ref):
    core = lax.rem(lax.axis_index("seq"), 2)
    rows, cols = tri(TOK, TOK)
    own_mask, lead_mask = rows <= cols, rows > cols
    for h in range(NH):
        k, v = head(kv_ref, h), head(kv_ref, h, 256)
        x, y, o = head(xb_ref, h), head(yo_ref, h), head(yo_ref, h, 256)
        xl, yl, ol = head(xl_ref, h), head(yol_ref, h), head(yol_ref, h, 256)

        def scores(left, own, lead):
            return jnp.concatenate(
                [jnp.where(own_mask, mm_nt(left, own), 0.0), jnp.where(lead_mask, mm_nt(left, lead), 0.0)], axis=1
            )

        a = scores(k, x, xl).astype(BF16)
        c = (scores(v, o, ol) - scores(k, y, yl)).astype(BF16)
        ys = jnp.concatenate([y, yl], axis=0)
        xs = jnp.concatenate([x, xl], axis=0)
        os = jnp.concatenate([o, ol], axis=0)
        gk_ref[:, h * DH : (h + 1) * DH] = mm(c, xs) - mm(a, ys)
        gv_ref[:, h * DH : (h + 1) * DH] = mm(a, os)
        pair = mm_tn(yl, xl)
        extra_ref[h] = jnp.where(core == 1, t_ref[h], pair + pair.T)
        extra_ref[NH + h] = jnp.where(core == 1, t_ref[NH + h], mm_tn(xl, ol))


def base_terms(kv_ref, part_ref, recv_ref, gk_in, gv_in, gk_ref, gv_ref):
    for h in range(NH):
        k, v = head(kv_ref, h), head(kv_ref, h, 256)
        s_hi, s_lo = split(part_ref[h] + recv_ref[h])
        c_hi, c_lo = split(part_ref[NH + h] + recv_ref[NH + h])
        cols = slice(h * DH, (h + 1) * DH)
        gk_ref[:, cols] = gk_in[:, cols] - mm(k, s_hi) - mm(k, s_lo) + mm_nt(v, c_hi) + mm_nt(v, c_lo)
        gv_ref[:, cols] = gv_in[:, cols] + mm(k, c_hi) + mm(k, c_lo)


def body(key_rows, values, d_layer, out_weight, saved_solutions, ridge_scale):
    n = lax.axis_size("seq")
    lag = n // 4

    def moved(value, source):
        route = [(source(i), i) for i in range(n) if source(i) is not None and 0 <= source(i) < n]
        return lax.ppermute(value, "seq", route)

    def swapped(value):
        return moved(value, lambda i: i ^ 1)

    st = (2 * NH, DH, DH)
    copies = jnp.broadcast_to(d_layer, (8, *d_layer.shape))
    gathered = lax.all_to_all(copies, "head", split_axis=0, concat_axis=0, tiled=True)

    own, kv, xb = call(
        own_states, [(st, F32), ((TOK, 512), BF16), ((TOK, 256), BF16)], key_rows, values, saved_solutions
    )
    kv_lag = moved(kv, lambda i: i - lag)
    x_lead = moved(xb, lambda i: i + lag)
    chip = own + swapped(own)
    p1 = moved(chip, lambda i: i - 2 if i % 2 == 0 else i - 4)
    p2 = moved(chip, lambda i: i - 6 if i % 2 == 0 else None)
    part, send = call(states_to_send, [(st, F32), (st, F32)], own, kv_lag, p1, p2)
    recv, x_lead = lax.optimization_barrier((swapped(send), x_lead))

    y, yo, tl = call(
        adjoints,
        [((TOK, 256), F32), ((TOK, 512), BF16), (st, F32)],
        gathered, out_weight, kv, kv_lag, saved_solutions, part, recv, ridge_scale,
        flops=1 << 32, smem=(7,),
    )

    yo_lead = moved(yo, lambda i: i + lag)
    chip_l = tl + swapped(tl)
    q1 = moved(chip_l, lambda i: i + 2 if i % 2 == 0 else i + 4)
    q2 = moved(chip_l, lambda i: i + 6 if i % 2 == 0 else None)
    gk, gv, extra = call(
        near_terms, [((TOK, 256), F32), ((TOK, 256), F32), (st, F32)], kv, xb, yo, x_lead, yo_lead, tl, flops=1 << 28
    )
    part_l = q1 + q2
    recv_l = swapped(part_l + extra)
    grad_k, grad_v = call(
        base_terms, [((TOK, 256), F32), ((TOK, 256), F32)], kv, part_l, recv_l, gk, gv
    )
    return y, grad_k, grad_v


def solution(mesh):
    return jax.shard_map(
        body,
        mesh=mesh,
        in_specs=(
            P("seq", "head"),
            P("seq", "head"),
            P("seq", "head"),
            P("head", None),
            P("seq", "head"),
            P("head"),
        ),
        out_specs=(P("seq", "head"), P("seq", "head"), P("seq", "head")),
        check_vma=False,
    )
```

```python
import jax
import jax.numpy as jnp
from jax import lax
from jax.experimental import pallas as pl
from jax.experimental.pallas import tpu as pltpu
from jax.sharding import PartitionSpec as P

DH = 128
TOK = 256
NH = 2
ITERS = 8
EPSILON = 1e-06
F32 = jnp.float32
BF16 = jnp.bfloat16
VM = pl.BlockSpec(memory_space=pltpu.VMEM)
SM = pl.BlockSpec(memory_space=pltpu.SMEM)
PARAMS = pltpu.CompilerParams(vmem_limit_bytes=24 * 1024 * 1024)


def mm(a, b):
    return lax.dot_general(a, b, (((1,), (0,)), ((), ())), preferred_element_type=F32)


def mm_nt(a, b):
    return lax.dot_general(a, b, (((1,), (1,)), ((), ())), preferred_element_type=F32)


def mm_tn(a, b):
    return lax.dot_general(a, b, (((0,), (0,)), ((), ())), preferred_element_type=F32)


def split(a):
    hi = a.astype(BF16)
    return hi, (a - hi.astype(F32)).astype(BF16)


def head(ref, h, base=0):
    return ref[:, base + h * DH : base + (h + 1) * DH]


def tri(rows, cols):
    r = lax.broadcasted_iota(jnp.int32, (rows, cols), 0)
    c = lax.broadcasted_iota(jnp.int32, (rows, cols), 1)
    return r, c


def call(kernel, outs, *args, flops=0, smem=()):
    return pl.pallas_call(
        kernel,
        out_shape=[jax.ShapeDtypeStruct(s, d) for s, d in outs],
        in_specs=[SM if i in smem else VM for i in range(len(args))],
        out_specs=[VM] * len(outs),
        compiler_params=PARAMS,
        cost_estimate=pl.CostEstimate(flops=flops, bytes_accessed=1 << 19, transcendentals=0),
    )(*args)


def own_states(k_ref, v_ref, t_ref, kv_ref):
    for h in range(NH):
        k = head(k_ref, h)
        t_ref[h] = mm_tn(k, k)
        t_ref[NH + h] = mm_tn(head(v_ref, h), k)
    kv_ref[:, : NH * DH] = k_ref[...]
    kv_ref[:, NH * DH :] = v_ref[...]


def to_forward(d_ref, up_ref, down_ref, x_ref, ridge_ref, a_ref, b_ref, c_ref, xb_ref, xlo_ref, rid_ref):
    core = lax.rem(lax.axis_index("seq"), 2)
    a_ref[0] = d_ref[...]
    a_ref[1] = up_ref[...]
    b_ref[0] = d_ref[...]
    b_ref[1] = down_ref[...]
    c_ref[...] = jnp.where(core == 0, up_ref[...], down_ref[...])
    xb_ref[...], xlo_ref[...] = split(x_ref[...])
    for h in range(NH):
        rid_ref[h] = jnp.full((8, DH), ridge_ref[h], F32)


def states_to_send(t_ref, lag_ref, p1_ref, p2_ref, part_ref, send_ref):
    core = lax.rem(lax.axis_index("seq"), 2)
    for h in range(NH):
        k = head(lag_ref, h)
        lag_g = mm_tn(k, k)
        lag_s = mm_tn(head(lag_ref, h, NH * DH), k)
        for at, lag in ((h, lag_g), (NH + h, lag_s)):
            part = p1_ref[at] + p2_ref[at]
            part_ref[at] = part
            send_ref[at] = part + jnp.where(core == 0, t_ref[at], lag)


def adjoints(
    d_ref, up_ref, down_ref, a_ref, b_ref, c_ref, w_ref, kv_ref, lag_ref, xb_ref, xlo_ref, part_ref, recv_ref, rid_ref,
    y_ref, yo_ref, t_ref,
):
    B = 128
    here = lax.axis_index("head")
    out = jnp.zeros((TOK, 256), F32)
    for away, chunk in (
        (0, d_ref[...]), (2, up_ref[...]), (6, down_ref[...]), (1, a_ref[0]),
        (3, a_ref[1]), (7, b_ref[0]), (5, b_ref[1]), (4, c_ref[...]),
    ):
        start = pl.multiple_of(lax.rem(here + away, 8) * 256, 256)
        out = out + mm_nt(chunk, w_ref[:, pl.ds(start, 256)])
    out = out.astype(BF16)
    yo_ref[:, 256:] = out
    rows, cols = tri(B, B)
    low, up = rows >= cols, rows < cols

    rhs, keys, ps, ridges = [], [], [], []
    for h in range(NH):
        k, v = head(kv_ref, h), head(kv_ref, h, 256)
        kl, vl = head(lag_ref, h), head(lag_ref, h, 256)
        gram = part_ref[h] + recv_ref[h]
        state = part_ref[NH + h] + recv_ref[NH + h]
        o = out[:, h * DH : (h + 1) * DH]
        for b in range(2):
            kb, vb = k[b * B : (b + 1) * B], v[b * B : (b + 1) * B]
            klb, vlb = kl[b * B : (b + 1) * B], vl[b * B : (b + 1) * B]
            ob = o[b * B : (b + 1) * B]
            kf, vf = (kl[B:], vl[B:]) if b == 0 else (k[:B], v[:B])
            g = gram + mm_tn(kf, kf)
            s = state + mm_tn(vf, kf)
            g_hi, g_lo = split(g)
            kbt = kb.astype(F32).T.astype(BF16)
            klbt = klb.astype(F32).T.astype(BF16)
            half = jnp.concatenate([g_hi, kbt, klbt, g_lo], axis=1)
            rhs.append(jnp.concatenate([half, half], axis=0))
            both = jnp.concatenate([kb, klb], axis=0)
            keys.append(jnp.concatenate([both, both], axis=0))
            sc = jnp.concatenate(
                [jnp.where(low, mm_nt(ob, vb), 0.0), jnp.where(up, mm_nt(ob, vlb), 0.0)], axis=1
            )
            sc_hi, sc_lo = split(sc)
            s_hi, s_lo = split(s)
            p = mm(ob, s_hi) + mm(ob, s_lo)
            p = p + mm(jnp.concatenate([sc_hi, sc_lo], axis=1), keys[-1])
            ps.append(p)
            ridges.append(rid_ref[h, :1])

    n = len(ps)

    def apply_gram(p, i):
        p_hi, p_lo = split(p)
        r = mm(jnp.concatenate([p_hi, p_lo], axis=1), rhs[i])
        sc = jnp.concatenate(
            [jnp.where(low, r[:, B : 2 * B], 0.0), jnp.where(up, r[:, 2 * B : 3 * B], 0.0)], axis=1
        )
        sc_hi, sc_lo = split(sc)
        t = mm(jnp.concatenate([sc_hi, sc_lo], axis=1), keys[i])
        return t + r[:, :B] + r[:, 3 * B :] + ridges[i] * p

    ys = [jnp.zeros((B, DH), F32)] * n
    rs = list(ps)
    rrs = [jnp.sum(r * r, axis=-1, keepdims=True) for r in rs]
    for it in range(ITERS):
        for i in range(n):
            a = apply_gram(ps[i], i)
            alpha = rrs[i] / (jnp.sum(ps[i] * a, axis=-1, keepdims=True) + EPSILON)
            ys[i] = ys[i] + alpha * ps[i]
            if it < ITERS - 1:
                rs[i] = rs[i] - alpha * a
                nr = jnp.sum(rs[i] * rs[i], axis=-1, keepdims=True)
                ps[i] = rs[i] + nr / (rrs[i] + EPSILON) * ps[i]
                rrs[i] = nr

    for h in range(NH):
        y = jnp.concatenate([ys[2 * h], ys[2 * h + 1]], axis=0)
        y_ref[:, h * DH : (h + 1) * DH] = y
        yo_ref[:, h * DH : (h + 1) * DH] = y.astype(BF16)
        y_hi, y_lo = split(y)
        x_hi, x_lo = head(xb_ref, h), head(xlo_ref, h)
        o = out[:, h * DH : (h + 1) * DH]
        pair = mm_tn(y_hi, x_hi) + mm_tn(y_lo, x_hi) + mm_tn(y_hi, x_lo)
        t_ref[h] = pair + pair.T
        t_ref[NH + h] = mm_tn(x_hi, o) + mm_tn(x_lo, o)


def pair_terms(k, v, x, y, o, mask):
    a = jnp.where(mask, mm_nt(k, x), 0.0).astype(BF16)
    c = jnp.where(mask, mm_nt(v, o) - mm_nt(k, y), 0.0).astype(BF16)
    return mm(c, x) - mm(a, y), mm(a, o)


def own_terms(kv_ref, xb_ref, yo_ref, gk_ref, gv_ref):
    rows, cols = tri(TOK, TOK)
    for h in range(NH):
        gk, gv = pair_terms(
            head(kv_ref, h), head(kv_ref, h, 256), head(xb_ref, h), head(yo_ref, h), head(yo_ref, h, 256), rows <= cols
        )
        gk_ref[:, h * DH : (h + 1) * DH] = gk
        gv_ref[:, h * DH : (h + 1) * DH] = gv


def early_terms(lag_ref, xb_ref, yo_ref, other_ref, early_ref):
    core = lax.rem(lax.axis_index("seq"), 2)
    rows, cols = tri(TOK, TOK)
    for h in range(NH):
        k, v = head(lag_ref, h), head(lag_ref, h, 256)
        gk, gv = pair_terms(k, v, head(xb_ref, h), head(yo_ref, h), head(yo_ref, h, 256), rows > cols)
        sym = jnp.where(core == 1, other_ref[h], 0.0).astype(BF16)
        cross = jnp.where(core == 1, other_ref[NH + h], 0.0).astype(BF16)
        gk = gk - mm(k, sym) + mm_nt(v, cross)
        early_ref[:, h * DH : (h + 1) * DH] = gk.astype(BF16)
        early_ref[:, 256 + h * DH : 256 + (h + 1) * DH] = (gv + mm(k, cross)).astype(BF16)


def base_terms(kv_ref, part_ref, recv_ref, early_ref, gk_in, gv_in, gk_ref, gv_ref):
    for h in range(NH):
        k, v = head(kv_ref, h), head(kv_ref, h, 256)
        s_hi, s_lo = split(part_ref[h] + recv_ref[h])
        c_hi, c_lo = split(part_ref[NH + h] + recv_ref[NH + h])
        cols = slice(h * DH, (h + 1) * DH)
        gk = gk_in[:, cols] + head(early_ref, h).astype(F32) - mm(k, s_hi) - mm(k, s_lo)
        gk_ref[:, cols] = gk + mm_nt(v, c_hi) + mm_nt(v, c_lo)
        gv_ref[:, cols] = gv_in[:, cols] + head(early_ref, h, 256).astype(F32) + mm(k, c_hi) + mm(k, c_lo)


def body(key_rows, values, d_layer, out_weight, saved_solutions, ridge_scale):
    n = lax.axis_size("seq")
    lag = n // 4

    def moved(value, source):
        route = [(source(i), i) for i in range(n) if source(i) is not None and 0 <= source(i) < n]
        return lax.ppermute(value, "seq", route)

    def swapped(value):
        return moved(value, lambda i: i ^ 1)

    st = (2 * NH, DH, DH)
    def around(value, away):
        return lax.ppermute(value, "head", [((i + away) % 8, i) for i in range(8)])

    up, down = around(d_layer, 2), around(d_layer, -2)
    own, kv = call(own_states, [(st, F32), ((TOK, 512), BF16)], key_rows, values)
    kv_lag = moved(kv, lambda i: i - lag)
    chip = own + swapped(own)
    pair = (2, TOK, 256)
    flat = ((TOK, 256), BF16)
    up_two, down_two, across, xb, xlo, rid = call(
        to_forward, [(pair, BF16), (pair, BF16), flat, flat, flat, ((NH, 8, DH), F32)],
        d_layer, up, down, saved_solutions, ridge_scale, flops=1 << 34, smem=(4,),
    )
    chip, up_two, down_two, across = lax.optimization_barrier((chip, up_two, down_two, across))
    up_two, down_two = around(up_two, 1), around(down_two, -1)
    far = [
        (s * 8 + (z + (2 if s % 2 == 0 else -2)) % 8, s * 8 + z) for s in range(n) for z in range(8)
    ]
    across = lax.ppermute(across, ("seq", "head"), far)
    p1 = moved(chip, lambda i: i - 2 if i % 2 == 0 else i - 4)
    p2 = moved(chip, lambda i: i - 6 if i % 2 == 0 else None)
    p1, p2, across, kv_lag = lax.optimization_barrier((p1, p2, across, kv_lag))
    part, send = call(states_to_send, [(st, F32), (st, F32)], own, kv_lag, p1, p2)
    recv = swapped(send)

    y, yo, tl = call(
        adjoints,
        [((TOK, 256), F32), ((TOK, 512), BF16), (st, F32)],
        d_layer, up, down, up_two, down_two, across, out_weight, kv, kv_lag, xb, xlo, part, recv, rid,
        flops=1 << 32,
    )

    other = swapped(tl)
    first = lax.rem(lax.axis_index("seq"), 2) == 0
    chip_l = (tl + other).astype(BF16)
    (early,) = call(early_terms, [((TOK, 512), BF16)], kv_lag, xb, yo, other, flops=1 << 26)
    early = moved(early, lambda i: i + lag)
    q1 = moved(chip_l, lambda i: i + 2 if i % 2 == 0 else i + 4)
    q2 = moved(chip_l, lambda i: i + 6 if i % 2 == 0 else None)
    gk, gv = call(own_terms, [((TOK, 256), F32)] * 2, kv, xb, yo, flops=1 << 26)
    both = q1.astype(F32) + q2.astype(F32)
    part_l = both + jnp.where(first, other, 0.0)
    recv_l = swapped(both)
    grad_k, grad_v = call(
        base_terms, [((TOK, 256), F32)] * 2, kv, part_l, recv_l, early, gk, gv
    )
    return y, grad_k, grad_v


def solution(mesh):
    return jax.shard_map(
        body,
        mesh=mesh,
        in_specs=(
            P("seq", "head"),
            P("seq", "head"),
            P("seq", "head"),
            P("head", None),
            P("seq", "head"),
            P("head"),
        ),
        out_specs=(P("seq", "head"), P("seq", "head"), P("seq", "head")),
        check_vma=False,
    )
```

```python
import jax
import jax.numpy as jnp
from jax import lax
from jax.experimental import pallas as pl
from jax.experimental.pallas import tpu as pltpu
from jax.sharding import PartitionSpec as P

DH = 128
TOK = 256
NH = 2
ITERS = 8
FINE = 3
EPSILON = 1e-06
F32 = jnp.float32
BF16 = jnp.bfloat16
VM = pl.BlockSpec(memory_space=pltpu.VMEM)
SM = pl.BlockSpec(memory_space=pltpu.SMEM)
PARAMS = pltpu.CompilerParams(vmem_limit_bytes=24 * 1024 * 1024)


def mm(a, b):
    return lax.dot_general(a, b, (((1,), (0,)), ((), ())), preferred_element_type=F32)


def mm_nt(a, b):
    return lax.dot_general(a, b, (((1,), (1,)), ((), ())), preferred_element_type=F32)


def mm_tn(a, b):
    return lax.dot_general(a, b, (((0,), (0,)), ((), ())), preferred_element_type=F32)


def split(a):
    hi = a.astype(BF16)
    return hi, (a - hi.astype(F32)).astype(BF16)


def head(ref, h, base=0):
    return ref[:, base + h * DH : base + (h + 1) * DH]


def tri(rows, cols):
    r = lax.broadcasted_iota(jnp.int32, (rows, cols), 0)
    c = lax.broadcasted_iota(jnp.int32, (rows, cols), 1)
    return r, c


def call(kernel, outs, *args, flops=0, size=1 << 19, smem=()):
    return pl.pallas_call(
        kernel,
        out_shape=[jax.ShapeDtypeStruct(s, d) for s, d in outs],
        in_specs=[SM if i in smem else VM for i in range(len(args))],
        out_specs=[VM] * len(outs),
        compiler_params=PARAMS,
        cost_estimate=pl.CostEstimate(flops=flops, bytes_accessed=size, transcendentals=0),
    )(*args)


def own_states(kvd_ref, t_ref, kv_ref, dv_ref):
    for h in range(NH):
        k = head(kvd_ref, h)
        t_ref[h] = mm_tn(k, k)
        t_ref[NH + h] = mm_tn(head(kvd_ref, h, 256), k)
    kv_ref[...] = kvd_ref[:, :512]
    dv_ref[...] = kvd_ref[:, 512:]


def to_forward(d_ref, up_ref, down_ref, x_ref, ridge_ref, a_ref, b_ref, c_ref, xb_ref, xlo_ref, rid_ref):
    core = lax.rem(lax.axis_index("seq"), 2)
    a_ref[0] = d_ref[...]
    a_ref[1] = up_ref[...]
    b_ref[0] = d_ref[...]
    b_ref[1] = down_ref[...]
    c_ref[...] = jnp.where(core == 0, up_ref[...], down_ref[...])
    xb_ref[...], xlo_ref[...] = split(x_ref[...])
    for h in range(NH):
        rid_ref[h] = jnp.full((8, DH), ridge_ref[h], F32)


def chip_states(own_ref, other_ref, out_ref):
    for h in range(NH):
        out_ref[h] = (own_ref[h] + other_ref[h]).astype(BF16)
        hi, lo = split(own_ref[NH + h] + other_ref[NH + h])
        out_ref[NH + h] = hi
        out_ref[2 * NH + h] = lo


def states_to_send(t_ref, lag_ref, p1_ref, p2_ref, part_ref, send_ref):
    core = lax.rem(lax.axis_index("seq"), 2)
    for h in range(NH):
        k = head(lag_ref, h)
        lag_g = mm_tn(k, k)
        lag_s = mm_tn(head(lag_ref, h, NH * DH), k)
        gram = p1_ref[h].astype(F32) + p2_ref[h].astype(F32)
        state = p1_ref[NH + h].astype(F32) + p2_ref[NH + h].astype(F32)
        state = state + p1_ref[2 * NH + h].astype(F32) + p2_ref[2 * NH + h].astype(F32)
        for at, lag, part in ((h, lag_g, gram), (NH + h, lag_s, state)):
            part_ref[at] = part
            send_ref[at] = part + jnp.where(core == 0, t_ref[at], lag)


def adjoints(
    d_ref, up_ref, down_ref, a_ref, b_ref, c_ref, w_ref, kv_ref, lag_ref, xb_ref, xlo_ref, part_ref, recv_ref, rid_ref,
    y_ref, yo_ref, t_ref,
):
    B = 128
    here = lax.axis_index("head")
    out = jnp.zeros((TOK, 256), F32)
    for away, chunk in (
        (0, d_ref[...]), (2, up_ref[...]), (6, down_ref[...]), (1, a_ref[0]),
        (3, a_ref[1]), (7, b_ref[0]), (5, b_ref[1]), (4, c_ref[...]),
    ):
        start = pl.multiple_of(lax.rem(here + away, 8) * 256, 256)
        out = out + mm_nt(chunk, w_ref[:, pl.ds(start, 256)])
    out = out.astype(BF16)
    yo_ref[:, 256:] = out
    rows, cols = tri(B, B)
    low, up = rows >= cols, rows < cols

    rhs, keys, ps, ridges = [], [], [], []
    for h in range(NH):
        k, v = head(kv_ref, h), head(kv_ref, h, 256)
        kl, vl = head(lag_ref, h), head(lag_ref, h, 256)
        gram = part_ref[h] + recv_ref[h]
        state = part_ref[NH + h] + recv_ref[NH + h]
        o = out[:, h * DH : (h + 1) * DH]
        for b in range(2):
            kb, vb = k[b * B : (b + 1) * B], v[b * B : (b + 1) * B]
            klb, vlb = kl[b * B : (b + 1) * B], vl[b * B : (b + 1) * B]
            ob = o[b * B : (b + 1) * B]
            kf, vf = (kl[B:], vl[B:]) if b == 0 else (k[:B], v[:B])
            g = gram + mm_tn(kf, kf)
            s = state + mm_tn(vf, kf)
            g_hi, g_lo = split(g)
            kbt = kb.astype(F32).T.astype(BF16)
            klbt = klb.astype(F32).T.astype(BF16)
            half = jnp.concatenate([g_hi, kbt, klbt, g_lo], axis=1)
            rhs.append(jnp.concatenate([half, half], axis=0))
            both = jnp.concatenate([kb, klb], axis=0)
            keys.append(jnp.concatenate([both, both], axis=0))
            sc = jnp.concatenate(
                [jnp.where(low, mm_nt(ob, vb), 0.0), jnp.where(up, mm_nt(ob, vlb), 0.0)], axis=1
            )
            sc_hi, sc_lo = split(sc)
            s_hi, s_lo = split(s)
            p = mm(ob, s_hi) + mm(ob, s_lo)
            p = p + mm(jnp.concatenate([sc_hi, sc_lo], axis=1), keys[-1])
            ps.append(p)
            ridges.append(rid_ref[h, :1])

    n = len(ps)

    def products(vectors, fine):
        firsts = []
        for i in range(n):
            if fine:
                hi, lo = split(vectors[i])
                firsts.append(mm(jnp.concatenate([hi, lo], axis=1), rhs[i]))
            else:
                firsts.append(mm(vectors[i].astype(BF16), rhs[i][:DH, : 3 * B]))
        seconds = []
        for i in range(n):
            r = firsts[i]
            sc = jnp.concatenate(
                [jnp.where(low, r[:, B : 2 * B], 0.0), jnp.where(up, r[:, 2 * B : 3 * B], 0.0)], axis=1
            )
            if fine:
                sc_hi, sc_lo = split(sc)
                seconds.append(mm(jnp.concatenate([sc_hi, sc_lo], axis=1), keys[i]))
            else:
                seconds.append(mm(sc.astype(BF16), keys[i][: 2 * B]))
        images = []
        for i in range(n):
            base = firsts[i][:, :B] + ridges[i] * vectors[i]
            if fine:
                base = base + firsts[i][:, 3 * B :]
            images.append(seconds[i] + base)
        return images

    ys = [jnp.zeros((B, DH), F32)] * n
    rs = list(ps)
    rrs = [jnp.sum(r * r, axis=-1, keepdims=True) for r in rs]
    images = products(ps, True)
    for it in range(ITERS):
        steps = [jnp.sum(ps[i] * images[i], axis=-1, keepdims=True) for i in range(n)]
        alphas = [rrs[i] / (steps[i] + EPSILON) for i in range(n)]
        rs = [rs[i] - alphas[i] * images[i] for i in range(n)]
        ys = [ys[i] + alphas[i] * ps[i] for i in range(n)]
        if it < ITERS - 1:
            fresh = products(rs, it + 1 < FINE)
            nrs = [jnp.sum(r * r, axis=-1, keepdims=True) for r in rs]
            betas = [nrs[i] / (rrs[i] + EPSILON) for i in range(n)]
            ps = [rs[i] + betas[i] * ps[i] for i in range(n)]
            images = [fresh[i] + betas[i] * images[i] for i in range(n)]
            rrs = nrs

    for h in range(NH):
        y = jnp.concatenate([ys[2 * h], ys[2 * h + 1]], axis=0)
        y_ref[:, h * DH : (h + 1) * DH] = y
        yo_ref[:, h * DH : (h + 1) * DH] = y.astype(BF16)
        y_hi, y_lo = split(y)
        x_hi, x_lo = head(xb_ref, h), head(xlo_ref, h)
        o = out[:, h * DH : (h + 1) * DH]
        pair = mm_tn(y_hi, x_hi) + mm_tn(y_lo, x_hi) + mm_tn(y_hi, x_lo)
        t_ref[h] = pair + pair.T
        t_ref[NH + h] = mm_tn(x_hi, o) + mm_tn(x_lo, o)


def pair_terms(k, v, x, y, o, mask):
    a = jnp.where(mask, mm_nt(k, x), 0.0).astype(BF16)
    c = jnp.where(mask, mm_nt(v, o) - mm_nt(k, y), 0.0).astype(BF16)
    return mm(c, x) - mm(a, y), mm(a, o)


def own_terms(kv_ref, xb_ref, yo_ref, gk_ref, gv_ref):
    rows, cols = tri(TOK, TOK)
    for h in range(NH):
        gk, gv = pair_terms(
            head(kv_ref, h), head(kv_ref, h, 256), head(xb_ref, h), head(yo_ref, h), head(yo_ref, h, 256), rows <= cols
        )
        gk_ref[:, h * DH : (h + 1) * DH] = gk
        gv_ref[:, h * DH : (h + 1) * DH] = gv


def early_terms(lag_ref, xb_ref, yo_ref, other_ref, early_ref):
    core = lax.rem(lax.axis_index("seq"), 2)
    rows, cols = tri(TOK, TOK)
    for h in range(NH):
        k, v = head(lag_ref, h), head(lag_ref, h, 256)
        gk, gv = pair_terms(k, v, head(xb_ref, h), head(yo_ref, h), head(yo_ref, h, 256), rows > cols)
        sym = jnp.where(core == 1, other_ref[h], 0.0).astype(BF16)
        cross = jnp.where(core == 1, other_ref[NH + h], 0.0).astype(BF16)
        gk = gk - mm(k, sym) + mm_nt(v, cross)
        early_ref[:, h * DH : (h + 1) * DH] = gk.astype(BF16)
        early_ref[:, 256 + h * DH : 256 + (h + 1) * DH] = (gv + mm(k, cross)).astype(BF16)


def base_terms(kv_ref, part_ref, recv_ref, early_ref, gk_in, gv_in, gk_ref, gv_ref):
    for h in range(NH):
        k, v = head(kv_ref, h), head(kv_ref, h, 256)
        s_hi, s_lo = split(part_ref[h] + recv_ref[h])
        c_hi, c_lo = split(part_ref[NH + h] + recv_ref[NH + h])
        cols = slice(h * DH, (h + 1) * DH)
        gk = gk_in[:, cols] + head(early_ref, h).astype(F32) - mm(k, s_hi) - mm(k, s_lo)
        gk_ref[:, cols] = gk + mm_nt(v, c_hi) + mm_nt(v, c_lo)
        gv_ref[:, cols] = gv_in[:, cols] + head(early_ref, h, 256).astype(F32) + mm(k, c_hi) + mm(k, c_lo)


def body(key_rows, values, d_layer, out_weight, saved_solutions, ridge_scale):
    n = lax.axis_size("seq")
    lag = n // 4

    def moved(value, source):
        route = [(source(i), i) for i in range(n) if source(i) is not None and 0 <= source(i) < n]
        return lax.ppermute(value, "seq", route)

    def swapped(value):
        return moved(value, lambda i: i ^ 1)

    st = (2 * NH, DH, DH)
    def around(value, away):
        return lax.ppermute(value, "head", [((i + away) % 8, i) for i in range(8)])

    up, down = around(d_layer, 2), around(d_layer, -2)
    flat = ((TOK, 256), BF16)
    kvd = jnp.concatenate([key_rows, values, d_layer], axis=1)
    own, kv, dv = call(own_states, [(st, F32), ((TOK, 512), BF16), flat], kvd)
    kv_lag = moved(kv, lambda i: i - lag)
    (chip,) = call(chip_states, [((3 * NH, DH, DH), BF16)], own, swapped(own))
    pair = (2, TOK, 256)
    up_two, down_two, across, xb, xlo, rid = call(
        to_forward, [(pair, BF16), (pair, BF16), flat, flat, flat, ((NH, 8, DH), F32)],
        dv, up, down, saved_solutions, ridge_scale, flops=1 << 34, smem=(4,),
    )
    up_two, down_two = around(up_two, 1), around(down_two, -1)
    far = [
        (s * 8 + (z + (2 if s % 2 == 0 else -2)) % 8, s * 8 + z) for s in range(n) for z in range(8)
    ]
    across = lax.ppermute(across, ("seq", "head"), far)
    p1 = moved(chip, lambda i: i - 2 if i % 2 == 0 else i - 4)
    p2 = moved(chip, lambda i: i - 6 if i % 2 == 0 else None)
    p1, p2, kv_lag = lax.optimization_barrier((p1, p2, kv_lag))
    part, send = call(states_to_send, [(st, F32), (st, F32)], own, kv_lag, p1, p2, size=0)
    send, across = lax.optimization_barrier((send, across))
    recv = swapped(send)

    y, yo, tl = call(
        adjoints,
        [((TOK, 256), F32), ((TOK, 512), BF16), (st, F32)],
        dv, up, down, up_two, down_two, across, out_weight, kv, kv_lag, xb, xlo, part, recv, rid,
        flops=1 << 32,
    )

    other = swapped(tl)
    first = lax.rem(lax.axis_index("seq"), 2) == 0
    chip_l = (tl + other).astype(BF16)
    (early,) = call(early_terms, [((TOK, 512), BF16)], kv_lag, xb, yo, other, flops=1 << 26)
    early = moved(early, lambda i: i + lag)
    q1 = moved(chip_l, lambda i: i + 2 if i % 2 == 0 else i + 4)
    q2 = moved(chip_l, lambda i: i + 6 if i % 2 == 0 else None)
    gk, gv = call(own_terms, [((TOK, 256), F32)] * 2, kv, xb, yo, flops=1 << 26)
    both = q1.astype(F32) + q2.astype(F32)
    part_l = both + jnp.where(first, other, 0.0)
    recv_l = swapped(both)
    grad_k, grad_v = call(
        base_terms, [((TOK, 256), F32)] * 2, kv, part_l, recv_l, early, gk, gv
    )
    return y, grad_k, grad_v


def solution(mesh):
    return jax.shard_map(
        body,
        mesh=mesh,
        in_specs=(
            P("seq", "head"),
            P("seq", "head"),
            P("seq", "head"),
            P("head", None),
            P("seq", "head"),
            P("head"),
        ),
        out_specs=(P("seq", "head"), P("seq", "head"), P("seq", "head")),
        check_vma=False,
    )
```

```python
import jax
import jax.numpy as jnp
from jax import lax
from jax.experimental import pallas as pl
from jax.experimental.pallas import tpu as pltpu
from jax.sharding import PartitionSpec as P

DH = 128
TOK = 256
NH = 2
ITERS = 8
FINE = 3
EPSILON = 1e-06
F32 = jnp.float32
BF16 = jnp.bfloat16
VM = pl.BlockSpec(memory_space=pltpu.VMEM)
SM = pl.BlockSpec(memory_space=pltpu.SMEM)
PARAMS = pltpu.CompilerParams(vmem_limit_bytes=24 * 1024 * 1024)


def mm(a, b):
    return lax.dot_general(a, b, (((1,), (0,)), ((), ())), preferred_element_type=F32)


def mm_nt(a, b):
    return lax.dot_general(a, b, (((1,), (1,)), ((), ())), preferred_element_type=F32)


def mm_tn(a, b):
    return lax.dot_general(a, b, (((0,), (0,)), ((), ())), preferred_element_type=F32)


def split(a):
    hi = a.astype(BF16)
    return hi, (a - hi.astype(F32)).astype(BF16)


def head(ref, h, base=0):
    return ref[:, base + h * DH : base + (h + 1) * DH]


def tri(rows, cols):
    r = lax.broadcasted_iota(jnp.int32, (rows, cols), 0)
    c = lax.broadcasted_iota(jnp.int32, (rows, cols), 1)
    return r, c


def call(kernel, outs, *args, flops=0, size=1 << 19, smem=()):
    return pl.pallas_call(
        kernel,
        out_shape=[jax.ShapeDtypeStruct(s, d) for s, d in outs],
        in_specs=[SM if i in smem else VM for i in range(len(args))],
        out_specs=[VM] * len(outs),
        compiler_params=PARAMS,
        cost_estimate=pl.CostEstimate(flops=flops, bytes_accessed=size, transcendentals=0),
    )(*args)


def own_states(kvd_ref, t_ref, kv_ref, dv_ref):
    for h in range(NH):
        k = head(kvd_ref, h)
        t_ref[h] = mm_tn(k, k)
        t_ref[NH + h] = mm_tn(head(kvd_ref, h, 256), k)
    kv_ref[...] = kvd_ref[:, :512]
    dv_ref[...] = kvd_ref[:, 512:]


def to_forward(d_ref, up_ref, down_ref, a_ref, b_ref, c_ref):
    core = lax.rem(lax.axis_index("seq"), 2)
    a_ref[0] = d_ref[...]
    a_ref[1] = up_ref[...]
    b_ref[0] = d_ref[...]
    b_ref[1] = down_ref[...]
    c_ref[...] = jnp.where(core == 0, up_ref[...], down_ref[...])


def weight_part(w_ref, away):
    start = pl.multiple_of(lax.rem(lax.axis_index("head") + away, 8) * 256, 256)
    return w_ref[:, pl.ds(start, 256)]


def halves(ref, h, base=0):
    whole = head(ref, h, base)
    return whole[:DH], whole[DH:]


def chip_states(own_ref, other_ref, out_ref):
    for h in range(NH):
        out_ref[h] = (own_ref[h] + other_ref[h]).astype(BF16)
        hi, lo = split(own_ref[NH + h] + other_ref[NH + h])
        out_ref[NH + h] = hi
        out_ref[2 * NH + h] = lo


def states_to_send(
    t_ref, lag_ref, p1_ref, p2_ref, kv_ref, d_ref, up_ref, down_ref, w_ref, x_ref, ridge_ref,
    part_ref, send_ref, out_ref, turned_ref, near_ref, xb_ref, xlo_ref, rid_ref,
):
    core = lax.rem(lax.axis_index("seq"), 2)
    for h in range(NH):
        k = head(lag_ref, h)
        lag_g = mm_tn(k, k)
        lag_s = mm_tn(head(lag_ref, h, NH * DH), k)
        gram = p1_ref[h].astype(F32) + p2_ref[h].astype(F32)
        state = p1_ref[NH + h].astype(F32) + p2_ref[NH + h].astype(F32)
        state = state + p1_ref[2 * NH + h].astype(F32) + p2_ref[2 * NH + h].astype(F32)
        for at, lag, part in ((h, lag_g, gram), (NH + h, lag_s, state)):
            part_ref[at] = part
            send_ref[at] = part + jnp.where(core == 0, t_ref[at], lag)
    out = mm_nt(d_ref[...], weight_part(w_ref, 0)) + mm_nt(up_ref[...], weight_part(w_ref, 2))
    out_ref[...] = out + mm_nt(down_ref[...], weight_part(w_ref, 6))
    for h in range(NH):
        keys, lags = halves(kv_ref, h), halves(lag_ref, h)
        for b in range(2):
            turned_ref[2 * h + b, :, :DH] = keys[b].astype(F32).T.astype(BF16)
            turned_ref[2 * h + b, :, DH:] = lags[b].astype(F32).T.astype(BF16)
        near_ref[4 * h] = mm_tn(lags[1], lags[1])
        near_ref[4 * h + 1] = mm_tn(keys[0], keys[0])
        near_ref[4 * h + 2] = mm_tn(halves(lag_ref, h, 256)[1], lags[1])
        near_ref[4 * h + 3] = mm_tn(halves(kv_ref, h, 256)[0], keys[0])
        rid_ref[h] = jnp.full((8, DH), ridge_ref[h], F32)
    xb_ref[...], xlo_ref[...] = split(x_ref[...])


def adjoints(
    a_ref, b_ref, c_ref, w_ref, kv_ref, lag_ref, xb_ref, xlo_ref, part_ref, recv_ref, rid_ref, out_ref, turned_ref,
    near_ref, y_ref, yo_ref, t_ref,
):
    B = 128
    out = out_ref[...]
    for away, chunk in ((4, c_ref[...]), (1, a_ref[0]), (3, a_ref[1]), (7, b_ref[0]), (5, b_ref[1])):
        out = out + mm_nt(chunk, weight_part(w_ref, away))
    out = out.astype(BF16)
    yo_ref[:, 256:] = out
    rows, cols = tri(B, B)
    low, up = rows >= cols, rows < cols

    rhs, keys, ps, ridges = [], [], [], []
    for h in range(NH):
        k, v = head(kv_ref, h), head(kv_ref, h, 256)
        kl, vl = head(lag_ref, h), head(lag_ref, h, 256)
        gram = part_ref[h] + recv_ref[h]
        state = part_ref[NH + h] + recv_ref[NH + h]
        o = out[:, h * DH : (h + 1) * DH]
        for b in range(2):
            kb, vb = k[b * B : (b + 1) * B], v[b * B : (b + 1) * B]
            klb, vlb = kl[b * B : (b + 1) * B], vl[b * B : (b + 1) * B]
            ob = o[b * B : (b + 1) * B]
            g = gram + near_ref[4 * h + b]
            s = state + near_ref[4 * h + 2 + b]
            g_hi, g_lo = split(g)
            half = jnp.concatenate([g_hi, turned_ref[2 * h + b], g_lo], axis=1)
            rhs.append(jnp.concatenate([half, half], axis=0))
            both = jnp.concatenate([kb, klb], axis=0)
            keys.append(jnp.concatenate([both, both], axis=0))
            sc = jnp.concatenate(
                [jnp.where(low, mm_nt(ob, vb), 0.0), jnp.where(up, mm_nt(ob, vlb), 0.0)], axis=1
            )
            sc_hi, sc_lo = split(sc)
            s_hi, s_lo = split(s)
            p = mm(ob, s_hi) + mm(ob, s_lo)
            p = p + mm(jnp.concatenate([sc_hi, sc_lo], axis=1), keys[-1])
            ps.append(p)
            ridges.append(rid_ref[h, :1])

    n = len(ps)

    def products(vectors, fine):
        firsts = []
        for i in range(n):
            if fine:
                hi, lo = split(vectors[i])
                firsts.append(mm(jnp.concatenate([hi, lo], axis=1), rhs[i]))
            else:
                firsts.append(mm(vectors[i].astype(BF16), rhs[i][:DH, : 3 * B]))
        seconds = []
        for i in range(n):
            r = firsts[i]
            sc = jnp.concatenate(
                [jnp.where(low, r[:, B : 2 * B], 0.0), jnp.where(up, r[:, 2 * B : 3 * B], 0.0)], axis=1
            )
            if fine:
                sc_hi, sc_lo = split(sc)
                seconds.append(mm(jnp.concatenate([sc_hi, sc_lo], axis=1), keys[i]))
            else:
                seconds.append(mm(sc.astype(BF16), keys[i][: 2 * B]))
        images = []
        for i in range(n):
            base = firsts[i][:, :B] + ridges[i] * vectors[i]
            if fine:
                base = base + firsts[i][:, 3 * B :]
            images.append(seconds[i] + base)
        return images

    ys = [jnp.zeros((B, DH), F32)] * n
    rs = list(ps)
    rrs = [jnp.sum(r * r, axis=-1, keepdims=True) for r in rs]
    images = products(ps, True)
    for it in range(ITERS):
        steps = [jnp.sum(ps[i] * images[i], axis=-1, keepdims=True) for i in range(n)]
        alphas = [rrs[i] / (steps[i] + EPSILON) for i in range(n)]
        rs = [rs[i] - alphas[i] * images[i] for i in range(n)]
        ys = [ys[i] + alphas[i] * ps[i] for i in range(n)]
        if it < ITERS - 1:
            fresh = products(rs, it + 1 < FINE)
            nrs = [jnp.sum(r * r, axis=-1, keepdims=True) for r in rs]
            betas = [nrs[i] / (rrs[i] + EPSILON) for i in range(n)]
            ps = [rs[i] + betas[i] * ps[i] for i in range(n)]
            images = [fresh[i] + betas[i] * images[i] for i in range(n)]
            rrs = nrs

    for h in range(NH):
        y = jnp.concatenate([ys[2 * h], ys[2 * h + 1]], axis=0)
        y_ref[:, h * DH : (h + 1) * DH] = y
        yo_ref[:, h * DH : (h + 1) * DH] = y.astype(BF16)
        y_hi, y_lo = split(y)
        x_hi, x_lo = head(xb_ref, h), head(xlo_ref, h)
        o = out[:, h * DH : (h + 1) * DH]
        pair = mm_tn(y_hi, x_hi) + mm_tn(y_lo, x_hi) + mm_tn(y_hi, x_lo)
        t_ref[h] = pair + pair.T
        t_ref[NH + h] = mm_tn(x_hi, o) + mm_tn(x_lo, o)


def pair_terms(k, v, x, y, o, mask):
    a = jnp.where(mask, mm_nt(k, x), 0.0).astype(BF16)
    c = jnp.where(mask, mm_nt(v, o) - mm_nt(k, y), 0.0).astype(BF16)
    return mm(c, x) - mm(a, y), mm(a, o)


def own_terms(kv_ref, xb_ref, yo_ref, gk_ref, gv_ref):
    rows, cols = tri(TOK, TOK)
    for h in range(NH):
        gk, gv = pair_terms(
            head(kv_ref, h), head(kv_ref, h, 256), head(xb_ref, h), head(yo_ref, h), head(yo_ref, h, 256), rows <= cols
        )
        gk_ref[:, h * DH : (h + 1) * DH] = gk
        gv_ref[:, h * DH : (h + 1) * DH] = gv


def early_terms(lag_ref, xb_ref, yo_ref, other_ref, early_ref):
    core = lax.rem(lax.axis_index("seq"), 2)
    rows, cols = tri(TOK, TOK)
    for h in range(NH):
        k, v = head(lag_ref, h), head(lag_ref, h, 256)
        gk, gv = pair_terms(k, v, head(xb_ref, h), head(yo_ref, h), head(yo_ref, h, 256), rows > cols)
        sym = jnp.where(core == 1, other_ref[h], 0.0).astype(BF16)
        cross = jnp.where(core == 1, other_ref[NH + h], 0.0).astype(BF16)
        gk = gk - mm(k, sym) + mm_nt(v, cross)
        early_ref[:, h * DH : (h + 1) * DH] = gk.astype(BF16)
        early_ref[:, 256 + h * DH : 256 + (h + 1) * DH] = (gv + mm(k, cross)).astype(BF16)


def base_terms(kv_ref, part_ref, recv_ref, early_ref, gk_in, gv_in, gk_ref, gv_ref):
    for h in range(NH):
        k, v = head(kv_ref, h), head(kv_ref, h, 256)
        s_hi, s_lo = split(part_ref[h] + recv_ref[h])
        c_hi, c_lo = split(part_ref[NH + h] + recv_ref[NH + h])
        cols = slice(h * DH, (h + 1) * DH)
        gk = gk_in[:, cols] + head(early_ref, h).astype(F32) - mm(k, s_hi) - mm(k, s_lo)
        gk_ref[:, cols] = gk + mm_nt(v, c_hi) + mm_nt(v, c_lo)
        gv_ref[:, cols] = gv_in[:, cols] + head(early_ref, h, 256).astype(F32) + mm(k, c_hi) + mm(k, c_lo)


def body(key_rows, values, d_layer, out_weight, saved_solutions, ridge_scale):
    n = lax.axis_size("seq")
    lag = n // 4

    def moved(value, source):
        route = [(source(i), i) for i in range(n) if source(i) is not None and 0 <= source(i) < n]
        return lax.ppermute(value, "seq", route)

    def swapped(value):
        return moved(value, lambda i: i ^ 1)

    st = (2 * NH, DH, DH)
    def around(value, away):
        return lax.ppermute(value, "head", [((i + away) % 8, i) for i in range(8)])

    up, down = around(d_layer, 2), around(d_layer, -2)
    flat = ((TOK, 256), BF16)
    kvd = jnp.concatenate([key_rows, values, d_layer], axis=1)
    own, kv, dv = call(own_states, [(st, F32), ((TOK, 512), BF16), flat], kvd)
    kv_lag = moved(kv, lambda i: i - lag)
    (chip,) = call(chip_states, [((3 * NH, DH, DH), BF16)], own, swapped(own))
    pair = (2, TOK, 256)
    up_two, down_two, across = call(
        to_forward, [(pair, BF16), (pair, BF16), flat], dv, up, down, flops=1 << 34
    )
    up_two, down_two = around(up_two, 1), around(down_two, -1)
    far = [
        (s * 8 + (z + (2 if s % 2 == 0 else -2)) % 8, s * 8 + z) for s in range(n) for z in range(8)
    ]
    across = lax.ppermute(across, ("seq", "head"), far)
    p1 = moved(chip, lambda i: i - 2 if i % 2 == 0 else i - 4)
    p2 = moved(chip, lambda i: i - 6 if i % 2 == 0 else None)
    p1, p2, kv_lag = lax.optimization_barrier((p1, p2, kv_lag))
    part, send, begun, turned, near, xb, xlo, rid = call(
        states_to_send,
        [
            (st, F32), (st, F32), ((TOK, 256), F32), ((4, DH, 256), BF16), ((8, DH, DH), F32), flat, flat,
            ((NH, 8, DH), F32),
        ],
        own, kv_lag, p1, p2, kv, dv, up, down, out_weight, saved_solutions, ridge_scale, size=0, smem=(10,),
    )
    send, across = lax.optimization_barrier((send, across))
    recv = swapped(send)

    y, yo, tl = call(
        adjoints,
        [((TOK, 256), F32), ((TOK, 512), BF16), (st, F32)],
        up_two, down_two, across, out_weight, kv, kv_lag, xb, xlo, part, recv, rid, begun, turned, near,
        flops=1 << 32,
    )

    other = swapped(tl)
    first = lax.rem(lax.axis_index("seq"), 2) == 0
    chip_l = (tl + other).astype(BF16)
    (early,) = call(early_terms, [((TOK, 512), BF16)], kv_lag, xb, yo, other, flops=1 << 26)
    early = moved(early, lambda i: i + lag)
    q1 = moved(chip_l, lambda i: i + 2 if i % 2 == 0 else i + 4)
    q2 = moved(chip_l, lambda i: i + 6 if i % 2 == 0 else None)
    gk, gv = call(own_terms, [((TOK, 256), F32)] * 2, kv, xb, yo, flops=1 << 26)
    both = q1.astype(F32) + q2.astype(F32)
    part_l = both + jnp.where(first, other, 0.0)
    recv_l = swapped(both)
    grad_k, grad_v = call(
        base_terms, [((TOK, 256), F32)] * 2, kv, part_l, recv_l, early, gk, gv
    )
    return y, grad_k, grad_v


def solution(mesh):
    return jax.shard_map(
        body,
        mesh=mesh,
        in_specs=(
            P("seq", "head"),
            P("seq", "head"),
            P("seq", "head"),
            P("head", None),
            P("seq", "head"),
            P("head"),
        ),
        out_specs=(P("seq", "head"), P("seq", "head"), P("seq", "head")),
        check_vma=False,
    )
```

```python
import jax
import jax.numpy as jnp
from jax import lax
from jax.experimental import pallas as pl
from jax.experimental.pallas import tpu as pltpu
from jax.sharding import PartitionSpec as P

DH = 128
TOK = 256
NH = 2
ITERS = 8
FINE = 3
EPSILON = 1e-06
F32 = jnp.float32
BF16 = jnp.bfloat16
VM = pl.BlockSpec(memory_space=pltpu.VMEM)
SM = pl.BlockSpec(memory_space=pltpu.SMEM)
PARAMS = pltpu.CompilerParams(vmem_limit_bytes=24 * 1024 * 1024)


def mm(a, b):
    return lax.dot_general(a, b, (((1,), (0,)), ((), ())), preferred_element_type=F32)


def mm_nt(a, b):
    return lax.dot_general(a, b, (((1,), (1,)), ((), ())), preferred_element_type=F32)


def mm_tn(a, b):
    return lax.dot_general(a, b, (((0,), (0,)), ((), ())), preferred_element_type=F32)


def split(a):
    hi = a.astype(BF16)
    return hi, (a - hi.astype(F32)).astype(BF16)


def head(ref, h, base=0):
    return ref[:, base + h * DH : base + (h + 1) * DH]


def tri(rows, cols):
    r = lax.broadcasted_iota(jnp.int32, (rows, cols), 0)
    c = lax.broadcasted_iota(jnp.int32, (rows, cols), 1)
    return r, c


def call(kernel, outs, *args, flops=0, size=1 << 19, smem=()):
    return pl.pallas_call(
        kernel,
        out_shape=[jax.ShapeDtypeStruct(s, d) for s, d in outs],
        in_specs=[SM if i in smem else VM for i in range(len(args))],
        out_specs=[VM] * len(outs),
        compiler_params=PARAMS,
        cost_estimate=pl.CostEstimate(flops=flops, bytes_accessed=size, transcendentals=0),
    )(*args)


def own_states(kvd_ref, t_ref, kv_ref, dv_ref):
    for h in range(NH):
        k = head(kvd_ref, h)
        t_ref[h] = mm_tn(k, k)
        t_ref[NH + h] = mm_tn(head(kvd_ref, h, 256), k)
    kv_ref[...] = kvd_ref[:, :512]
    dv_ref[...] = kvd_ref[:, 512:]


def to_forward(d_ref, up_ref, down_ref, a_ref, b_ref, c_ref):
    core = lax.rem(lax.axis_index("seq"), 2)
    a_ref[0] = d_ref[...]
    a_ref[1] = up_ref[...]
    b_ref[0] = d_ref[...]
    b_ref[1] = down_ref[...]
    c_ref[...] = jnp.where(core == 0, up_ref[...], down_ref[...])


def weight_part(w_ref, away):
    start = pl.multiple_of(lax.rem(lax.axis_index("head") + away, 8) * 256, 256)
    return w_ref[:, pl.ds(start, 256)]


def halves(ref, h, base=0):
    whole = head(ref, h, base)
    return whole[:DH], whole[DH:]


def chip_states(own_ref, other_ref, out_ref):
    for h in range(NH):
        out_ref[h] = (own_ref[h] + other_ref[h]).astype(BF16)
        hi, lo = split(own_ref[NH + h] + other_ref[NH + h])
        out_ref[NH + h] = hi
        out_ref[2 * NH + h] = lo


def states_to_send(
    t_ref, lag_ref, p1_ref, p2_ref, kv_ref, d_ref, up_ref, down_ref, w_ref, x_ref, ridge_ref,
    part_ref, send_ref, out_ref, turned_ref, near_ref, xb_ref, xlo_ref, rid_ref,
):
    core = lax.rem(lax.axis_index("seq"), 2)
    for h in range(NH):
        k = head(lag_ref, h)
        lag_g = mm_tn(k, k)
        lag_s = mm_tn(head(lag_ref, h, NH * DH), k)
        gram = p1_ref[h].astype(F32) + p2_ref[h].astype(F32)
        state = p1_ref[NH + h].astype(F32) + p2_ref[NH + h].astype(F32)
        state = state + p1_ref[2 * NH + h].astype(F32) + p2_ref[2 * NH + h].astype(F32)
        for at, lag, part in ((h, lag_g, gram), (NH + h, lag_s, state)):
            part_ref[at] = part
            send_ref[at] = part + jnp.where(core == 0, t_ref[at], lag)
    out = mm_nt(d_ref[...], weight_part(w_ref, 0)) + mm_nt(up_ref[...], weight_part(w_ref, 2))
    out_ref[...] = out + mm_nt(down_ref[...], weight_part(w_ref, 6))
    for h in range(NH):
        keys, lags = halves(kv_ref, h), halves(lag_ref, h)
        for b in range(2):
            turned_ref[2 * h + b, :, :DH] = keys[b].astype(F32).T.astype(BF16)
            turned_ref[2 * h + b, :, DH:] = lags[b].astype(F32).T.astype(BF16)
        near_ref[4 * h] = mm_tn(lags[1], lags[1])
        near_ref[4 * h + 1] = mm_tn(keys[0], keys[0])
        near_ref[4 * h + 2] = mm_tn(halves(lag_ref, h, 256)[1], lags[1])
        near_ref[4 * h + 3] = mm_tn(halves(kv_ref, h, 256)[0], keys[0])
        rid_ref[h] = jnp.full((8, DH), ridge_ref[h], F32)
    xb_ref[...], xlo_ref[...] = split(x_ref[...])


def adjoints(
    a_ref, b_ref, c_ref, w_ref, kv_ref, lag_ref, xb_ref, xlo_ref, part_ref, recv_ref, rid_ref, out_ref, turned_ref,
    near_ref, y_out, yo_ref, t_ref, y_ref, sems,
):
    B = 128
    out = out_ref[...]
    for away, chunk in ((4, c_ref[...]), (1, a_ref[0]), (3, a_ref[1]), (7, b_ref[0]), (5, b_ref[1])):
        out = out + mm_nt(chunk, weight_part(w_ref, away))
    out = out.astype(BF16)
    yo_ref[:, 256:] = out
    rows, cols = tri(B, B)
    low, up = rows >= cols, rows < cols

    rhs, keys, ps, ridges = [], [], [], []
    for h in range(NH):
        k, v = head(kv_ref, h), head(kv_ref, h, 256)
        kl, vl = head(lag_ref, h), head(lag_ref, h, 256)
        gram = part_ref[h] + recv_ref[h]
        state = part_ref[NH + h] + recv_ref[NH + h]
        o = out[:, h * DH : (h + 1) * DH]
        for b in range(2):
            kb, vb = k[b * B : (b + 1) * B], v[b * B : (b + 1) * B]
            klb, vlb = kl[b * B : (b + 1) * B], vl[b * B : (b + 1) * B]
            ob = o[b * B : (b + 1) * B]
            g = gram + near_ref[4 * h + b]
            s = state + near_ref[4 * h + 2 + b]
            g_hi, g_lo = split(g)
            half = jnp.concatenate([g_hi, turned_ref[2 * h + b], g_lo], axis=1)
            rhs.append(jnp.concatenate([half, half], axis=0))
            both = jnp.concatenate([kb, klb], axis=0)
            keys.append(jnp.concatenate([both, both], axis=0))
            sc = jnp.concatenate(
                [jnp.where(low, mm_nt(ob, vb), 0.0), jnp.where(up, mm_nt(ob, vlb), 0.0)], axis=1
            )
            sc_hi, sc_lo = split(sc)
            s_hi, s_lo = split(s)
            p = mm(ob, s_hi) + mm(ob, s_lo)
            p = p + mm(jnp.concatenate([sc_hi, sc_lo], axis=1), keys[-1])
            ps.append(p)
            ridges.append(rid_ref[h, :1])

    for h in range(NH):
        o = out[:, h * DH : (h + 1) * DH]
        t_ref[NH + h] = mm_tn(head(xb_ref, h), o) + mm_tn(head(xlo_ref, h), o)

    n = len(ps)

    def products(vectors, fine):
        firsts = []
        for i in range(n):
            if fine:
                hi, lo = split(vectors[i])
                firsts.append(mm(jnp.concatenate([hi, lo], axis=1), rhs[i]))
            else:
                firsts.append(mm(vectors[i].astype(BF16), rhs[i][:DH, : 3 * B]))
        seconds = []
        for i in range(n):
            r = firsts[i]
            sc = jnp.concatenate(
                [jnp.where(low, r[:, B : 2 * B], 0.0), jnp.where(up, r[:, 2 * B : 3 * B], 0.0)], axis=1
            )
            if fine:
                sc_hi, sc_lo = split(sc)
                seconds.append(mm(jnp.concatenate([sc_hi, sc_lo], axis=1), keys[i]))
            else:
                seconds.append(mm(sc.astype(BF16), keys[i][: 2 * B]))
        images = []
        for i in range(n):
            base = firsts[i][:, :B] + ridges[i] * vectors[i]
            if fine:
                base = base + firsts[i][:, 3 * B :]
            images.append(seconds[i] + base)
        return images

    ys = [jnp.zeros((B, DH), F32)] * n
    rs = list(ps)
    rrs = [jnp.sum(r * r, axis=-1, keepdims=True) for r in rs]
    images = products(ps, True)
    for it in range(ITERS):
        steps = [jnp.sum(ps[i] * images[i], axis=-1, keepdims=True) for i in range(n)]
        alphas = [rrs[i] / (steps[i] + EPSILON) for i in range(n)]
        rs = [rs[i] - alphas[i] * images[i] for i in range(n)]
        ys = [ys[i] + alphas[i] * ps[i] for i in range(n)]
        if it < ITERS - 1:
            fresh = products(rs, it + 1 < FINE)
            nrs = [jnp.sum(r * r, axis=-1, keepdims=True) for r in rs]
            betas = [nrs[i] / (rrs[i] + EPSILON) for i in range(n)]
            ps = [rs[i] + betas[i] * ps[i] for i in range(n)]
            images = [fresh[i] + betas[i] * images[i] for i in range(n)]
            rrs = nrs

    copies = []
    for h in range(NH):
        y = jnp.concatenate([ys[2 * h], ys[2 * h + 1]], axis=0)
        cols = slice(h * DH, (h + 1) * DH)
        y_ref[:, cols] = y
        copies.append(pltpu.make_async_copy(y_ref.at[:, cols], y_out.at[:, cols], sems.at[h]))
        copies[-1].start()
        yo_ref[:, h * DH : (h + 1) * DH] = y.astype(BF16)
        y_hi, y_lo = split(y)
        x_hi, x_lo = head(xb_ref, h), head(xlo_ref, h)
        pair = mm_tn(y_hi, x_hi) + mm_tn(y_lo, x_hi) + mm_tn(y_hi, x_lo)
        t_ref[h] = pair + pair.T
    for copy in copies:
        copy.wait()


def pair_terms(k, v, x, y, o, mask):
    a = jnp.where(mask, mm_nt(k, x), 0.0).astype(BF16)
    c = jnp.where(mask, mm_nt(v, o) - mm_nt(k, y), 0.0).astype(BF16)
    return mm(c, x) - mm(a, y), mm(a, o)


def own_terms(kv_ref, xb_ref, yo_ref, gk_ref, gv_ref):
    rows, cols = tri(TOK, TOK)
    for h in range(NH):
        gk, gv = pair_terms(
            head(kv_ref, h), head(kv_ref, h, 256), head(xb_ref, h), head(yo_ref, h), head(yo_ref, h, 256), rows <= cols
        )
        gk_ref[:, h * DH : (h + 1) * DH] = gk
        gv_ref[:, h * DH : (h + 1) * DH] = gv


def early_pairs(lag_ref, xb_ref, yo_ref, early_ref):
    rows, cols = tri(TOK, TOK)
    for h in range(NH):
        gk, gv = pair_terms(
            head(lag_ref, h), head(lag_ref, h, 256), head(xb_ref, h), head(yo_ref, h), head(yo_ref, h, 256), rows > cols
        )
        early_ref[:, h * DH : (h + 1) * DH] = gk.astype(BF16)
        early_ref[:, 256 + h * DH : 256 + (h + 1) * DH] = gv.astype(BF16)


def early_terms(lag_ref, pairs_ref, other_ref, early_ref):
    core = lax.rem(lax.axis_index("seq"), 2)
    for h in range(NH):
        k, v = head(lag_ref, h), head(lag_ref, h, 256)
        sym = jnp.where(core == 1, other_ref[h], 0.0).astype(BF16)
        cross = jnp.where(core == 1, other_ref[NH + h], 0.0).astype(BF16)
        gk = head(pairs_ref, h).astype(F32) - mm(k, sym) + mm_nt(v, cross)
        gv = head(pairs_ref, h, 256).astype(F32) + mm(k, cross)
        early_ref[:, h * DH : (h + 1) * DH] = gk.astype(BF16)
        early_ref[:, 256 + h * DH : 256 + (h + 1) * DH] = gv.astype(BF16)


def base_terms(kv_ref, part_ref, recv_ref, early_ref, gk_in, gv_in, gk_ref, gv_ref):
    for h in range(NH):
        k, v = head(kv_ref, h), head(kv_ref, h, 256)
        s_hi, s_lo = split(part_ref[h] + recv_ref[h])
        c_hi, c_lo = split(part_ref[NH + h] + recv_ref[NH + h])
        cols = slice(h * DH, (h + 1) * DH)
        gk = gk_in[:, cols] + head(early_ref, h).astype(F32) - mm(k, s_hi) - mm(k, s_lo)
        gk_ref[:, cols] = gk + mm_nt(v, c_hi) + mm_nt(v, c_lo)
        gv_ref[:, cols] = gv_in[:, cols] + head(early_ref, h, 256).astype(F32) + mm(k, c_hi) + mm(k, c_lo)


def body(key_rows, values, d_layer, out_weight, saved_solutions, ridge_scale):
    n = lax.axis_size("seq")
    lag = n // 4

    def moved(value, source):
        route = [(source(i), i) for i in range(n) if source(i) is not None and 0 <= source(i) < n]
        return lax.ppermute(value, "seq", route)

    def swapped(value):
        return moved(value, lambda i: i ^ 1)

    st = (2 * NH, DH, DH)
    def around(value, away):
        return lax.ppermute(value, "head", [((i + away) % 8, i) for i in range(8)])

    up, down = around(d_layer, 2), around(d_layer, -2)
    flat = ((TOK, 256), BF16)
    kvd = jnp.concatenate([key_rows, values, d_layer], axis=1)
    own, kv, dv = call(own_states, [(st, F32), ((TOK, 512), BF16), flat], kvd)
    kv_lag = moved(kv, lambda i: i - lag)
    (chip,) = call(chip_states, [((3 * NH, DH, DH), BF16)], own, swapped(own))
    pair = (2, TOK, 256)
    up_two, down_two, across = call(
        to_forward, [(pair, BF16), (pair, BF16), flat], dv, up, down, flops=1 << 34
    )
    up_two, down_two = around(up_two, 1), around(down_two, -1)
    far = [
        (s * 8 + (z + (2 if s % 2 == 0 else -2)) % 8, s * 8 + z) for s in range(n) for z in range(8)
    ]
    across = lax.ppermute(across, ("seq", "head"), far)
    p1 = moved(chip, lambda i: i - 2 if i % 2 == 0 else i - 4)
    p2 = moved(chip, lambda i: i - 6 if i % 2 == 0 else None)
    p1, p2, kv_lag = lax.optimization_barrier((p1, p2, kv_lag))
    part, send, begun, turned, near, xb, xlo, rid = call(
        states_to_send,
        [
            (st, F32), (st, F32), ((TOK, 256), F32), ((4, DH, 256), BF16), ((8, DH, DH), F32), flat, flat,
            ((NH, 8, DH), F32),
        ],
        own, kv_lag, p1, p2, kv, dv, up, down, out_weight, saved_solutions, ridge_scale, size=0, smem=(10,),
    )
    send, across = lax.optimization_barrier((send, across))
    recv = swapped(send)

    y, yo, tl = pl.pallas_call(
        adjoints,
        out_shape=[
            jax.ShapeDtypeStruct((TOK, 256), F32),
            jax.ShapeDtypeStruct((TOK, 512), BF16),
            jax.ShapeDtypeStruct(st, F32),
        ],
        in_specs=[VM] * 14,
        out_specs=[pl.BlockSpec(memory_space=pltpu.HBM), VM, VM],
        scratch_shapes=[pltpu.VMEM((TOK, 256), F32), pltpu.SemaphoreType.DMA((NH,))],
        compiler_params=PARAMS,
        cost_estimate=pl.CostEstimate(flops=1 << 32, bytes_accessed=1 << 19, transcendentals=0),
    )(up_two, down_two, across, out_weight, kv, kv_lag, xb, xlo, part, recv, rid, begun, turned, near)

    (pairs,) = call(early_pairs, [((TOK, 512), BF16)], kv_lag, xb, yo, flops=1 << 26)
    other, pairs = lax.optimization_barrier((swapped(tl), pairs))
    first = lax.rem(lax.axis_index("seq"), 2) == 0
    chip_l = (tl + other).astype(BF16)
    (early,) = call(early_terms, [((TOK, 512), BF16)], kv_lag, pairs, other, flops=1 << 26)
    early = moved(early, lambda i: i + lag)
    q1 = moved(chip_l, lambda i: i + 2 if i % 2 == 0 else i + 4)
    q2 = moved(chip_l, lambda i: i + 6 if i % 2 == 0 else None)
    gk, gv = call(own_terms, [((TOK, 256), F32)] * 2, kv, xb, yo, flops=1 << 26)
    both = q1.astype(F32) + q2.astype(F32)
    part_l = both + jnp.where(first, other, 0.0)
    recv_l = swapped(both)
    grad_k, grad_v = call(
        base_terms, [((TOK, 256), F32)] * 2, kv, part_l, recv_l, early, gk, gv
    )
    return y, grad_k, grad_v


def solution(mesh):
    return jax.shard_map(
        body,
        mesh=mesh,
        in_specs=(
            P("seq", "head"),
            P("seq", "head"),
            P("seq", "head"),
            P("head", None),
            P("seq", "head"),
            P("head"),
        ),
        out_specs=(P("seq", "head"), P("seq", "head"), P("seq", "head")),
        check_vma=False,
    )
```

```python
import jax
import jax.numpy as jnp
from jax import lax
from jax.experimental import pallas as pl
from jax.experimental.pallas import tpu as pltpu
from jax.sharding import PartitionSpec as P

DH = 128
TOK = 256
NH = 2
ITERS = 8
FINE = 3
EPSILON = 1e-06
F32 = jnp.float32
BF16 = jnp.bfloat16
VM = pl.BlockSpec(memory_space=pltpu.VMEM)
SM = pl.BlockSpec(memory_space=pltpu.SMEM)
PARAMS = pltpu.CompilerParams(vmem_limit_bytes=24 * 1024 * 1024)


def mm(a, b):
    return lax.dot_general(a, b, (((1,), (0,)), ((), ())), preferred_element_type=F32)


def mm_nt(a, b):
    return lax.dot_general(a, b, (((1,), (1,)), ((), ())), preferred_element_type=F32)


def mm_tn(a, b):
    return lax.dot_general(a, b, (((0,), (0,)), ((), ())), preferred_element_type=F32)


def split(a):
    hi = a.astype(BF16)
    return hi, (a - hi.astype(F32)).astype(BF16)


def head(ref, h, base=0):
    return ref[:, base + h * DH : base + (h + 1) * DH]


def tri(rows, cols):
    r = lax.broadcasted_iota(jnp.int32, (rows, cols), 0)
    c = lax.broadcasted_iota(jnp.int32, (rows, cols), 1)
    return r, c


def call(kernel, outs, *args, flops=0, size=1 << 19, smem=()):
    return pl.pallas_call(
        kernel,
        out_shape=[jax.ShapeDtypeStruct(s, d) for s, d in outs],
        in_specs=[SM if i in smem else VM for i in range(len(args))],
        out_specs=[VM] * len(outs),
        compiler_params=PARAMS,
        cost_estimate=pl.CostEstimate(flops=flops, bytes_accessed=size, transcendentals=0),
    )(*args)


def own_states(kvd_ref, t_ref, kv_ref, dv_ref):
    for h in range(NH):
        k = head(kvd_ref, h)
        t_ref[h] = mm_tn(k, k)
        t_ref[NH + h] = mm_tn(head(kvd_ref, h, 256), k)
    kv_ref[...] = kvd_ref[:, :512]
    dv_ref[...] = kvd_ref[:, 512:]


def to_forward(d_ref, up_ref, down_ref, a_ref, b_ref, c_ref):
    core = lax.rem(lax.axis_index("seq"), 2)
    a_ref[0] = d_ref[...]
    a_ref[1] = up_ref[...]
    b_ref[0] = d_ref[...]
    b_ref[1] = down_ref[...]
    c_ref[...] = jnp.where(core == 0, up_ref[...], down_ref[...])


def weight_part(w_ref, away):
    start = pl.multiple_of(lax.rem(lax.axis_index("head") + away, 8) * 256, 256)
    return w_ref[:, pl.ds(start, 256)]


def halves(ref, h, base=0):
    whole = head(ref, h, base)
    return whole[:DH], whole[DH:]


def chip_states(own_ref, other_ref, out_ref):
    for h in range(NH):
        out_ref[h] = (own_ref[h] + other_ref[h]).astype(BF16)
        hi, lo = split(own_ref[NH + h] + other_ref[NH + h])
        out_ref[NH + h] = hi
        out_ref[2 * NH + h] = lo


def states_to_send(
    t_ref, lag_ref, p1_ref, p2_ref, kv_ref, d_ref, up_ref, down_ref, w_ref, x_ref, ridge_ref,
    part_ref, send_ref, out_ref, turned_ref, near_ref, xb_ref, xlo_ref, rid_ref,
):
    core = lax.rem(lax.axis_index("seq"), 2)
    for h in range(NH):
        k = head(lag_ref, h)
        lag_g = mm_tn(k, k)
        lag_s = mm_tn(head(lag_ref, h, NH * DH), k)
        gram = p1_ref[h].astype(F32) + p2_ref[h].astype(F32)
        state = p1_ref[NH + h].astype(F32) + p2_ref[NH + h].astype(F32)
        state = state + p1_ref[2 * NH + h].astype(F32) + p2_ref[2 * NH + h].astype(F32)
        for at, lag, part in ((h, lag_g, gram), (NH + h, lag_s, state)):
            part_ref[at] = part
            send_ref[at] = part + jnp.where(core == 0, t_ref[at], lag)
    out = mm_nt(d_ref[...], weight_part(w_ref, 0)) + mm_nt(up_ref[...], weight_part(w_ref, 2))
    out_ref[...] = out + mm_nt(down_ref[...], weight_part(w_ref, 6))
    for h in range(NH):
        keys, lags = halves(kv_ref, h), halves(lag_ref, h)
        for b in range(2):
            turned_ref[2 * h + b, :, :DH] = keys[b].astype(F32).T.astype(BF16)
            turned_ref[2 * h + b, :, DH:] = lags[b].astype(F32).T.astype(BF16)
        near_ref[4 * h] = mm_tn(lags[1], lags[1])
        near_ref[4 * h + 1] = mm_tn(keys[0], keys[0])
        near_ref[4 * h + 2] = mm_tn(halves(lag_ref, h, 256)[1], lags[1])
        near_ref[4 * h + 3] = mm_tn(halves(kv_ref, h, 256)[0], keys[0])
        rid_ref[h] = jnp.full((8, DH), ridge_ref[h], F32)
    xb_ref[...], xlo_ref[...] = split(x_ref[...])


def adjoints(
    a_ref, b_ref, c_ref, w_ref, kv_ref, lag_ref, xb_ref, xlo_ref, part_ref, recv_ref, rid_ref, out_ref, turned_ref,
    near_ref, y_out, yo_ref, t_ref, y_ref, sems,
):
    B = 128
    out = out_ref[...]
    for away, chunk in ((4, c_ref[...]), (1, a_ref[0]), (3, a_ref[1]), (7, b_ref[0]), (5, b_ref[1])):
        out = out + mm_nt(chunk, weight_part(w_ref, away))
    out = out.astype(BF16)
    yo_ref[:, 256:] = out
    rows, cols = tri(B, B)
    low, up = rows >= cols, rows < cols

    rhs, keys, ps, ridges = [], [], [], []
    for h in range(NH):
        k, v = head(kv_ref, h), head(kv_ref, h, 256)
        kl, vl = head(lag_ref, h), head(lag_ref, h, 256)
        gram = part_ref[h] + recv_ref[h]
        state = part_ref[NH + h] + recv_ref[NH + h]
        o = out[:, h * DH : (h + 1) * DH]
        for b in range(2):
            kb, vb = k[b * B : (b + 1) * B], v[b * B : (b + 1) * B]
            klb, vlb = kl[b * B : (b + 1) * B], vl[b * B : (b + 1) * B]
            ob = o[b * B : (b + 1) * B]
            g = gram + near_ref[4 * h + b]
            s = state + near_ref[4 * h + 2 + b]
            g_hi, g_lo = split(g)
            half = jnp.concatenate([g_hi, turned_ref[2 * h + b], g_lo], axis=1)
            rhs.append(jnp.concatenate([half, half], axis=0))
            both = jnp.concatenate([kb, klb], axis=0)
            keys.append(jnp.concatenate([both, both], axis=0))
            sc = jnp.concatenate(
                [jnp.where(low, mm_nt(ob, vb), 0.0), jnp.where(up, mm_nt(ob, vlb), 0.0)], axis=1
            )
            sc_hi, sc_lo = split(sc)
            s_hi, s_lo = split(s)
            p = mm(ob, s_hi) + mm(ob, s_lo)
            p = p + mm(jnp.concatenate([sc_hi, sc_lo], axis=1), keys[-1])
            ps.append(p)
            ridges.append(rid_ref[h, :1])

    for h in range(NH):
        o = out[:, h * DH : (h + 1) * DH]
        t_ref[NH + h] = mm_tn(head(xb_ref, h), o) + mm_tn(head(xlo_ref, h), o)

    n = len(ps)

    def products(vectors, fine):
        firsts = []
        for i in range(n):
            if fine:
                hi, lo = split(vectors[i])
                firsts.append(mm(jnp.concatenate([hi, lo], axis=1), rhs[i]))
            else:
                firsts.append(mm(vectors[i].astype(BF16), rhs[i][:DH, : 3 * B]))
        seconds = []
        for i in range(n):
            r = firsts[i]
            sc = jnp.concatenate(
                [jnp.where(low, r[:, B : 2 * B], 0.0), jnp.where(up, r[:, 2 * B : 3 * B], 0.0)], axis=1
            )
            if fine:
                sc_hi, sc_lo = split(sc)
                seconds.append(mm(jnp.concatenate([sc_hi, sc_lo], axis=1), keys[i]))
            else:
                seconds.append(mm(sc.astype(BF16), keys[i][: 2 * B]))
        images = []
        for i in range(n):
            base = firsts[i][:, :B] + ridges[i] * vectors[i]
            if fine:
                base = base + firsts[i][:, 3 * B :]
            images.append(seconds[i] + base)
        return images

    ys = [jnp.zeros((B, DH), F32)] * n
    rs = list(ps)
    rrs = [jnp.sum(r * r, axis=-1, keepdims=True) for r in rs]
    images = products(ps, True)
    for it in range(ITERS):
        steps = [jnp.sum(ps[i] * images[i], axis=-1, keepdims=True) for i in range(n)]
        alphas = [rrs[i] / (steps[i] + EPSILON) for i in range(n)]
        rs = [rs[i] - alphas[i] * images[i] for i in range(n)]
        ys = [ys[i] + alphas[i] * ps[i] for i in range(n)]
        if it < ITERS - 1:
            fresh = products(rs, it + 1 < FINE)
            nrs = [jnp.sum(r * r, axis=-1, keepdims=True) for r in rs]
            betas = [nrs[i] / (rrs[i] + EPSILON) for i in range(n)]
            ps = [rs[i] + betas[i] * ps[i] for i in range(n)]
            images = [fresh[i] + betas[i] * images[i] for i in range(n)]
            rrs = nrs

    copies = []
    for h in range(NH):
        y = jnp.concatenate([ys[2 * h], ys[2 * h + 1]], axis=0)
        cols = slice(h * DH, (h + 1) * DH)
        y_ref[:, cols] = y
        copies.append(pltpu.make_async_copy(y_ref.at[:, cols], y_out.at[:, cols], sems.at[h]))
        copies[-1].start()
        yo_ref[:, h * DH : (h + 1) * DH] = y.astype(BF16)
        y_hi, y_lo = split(y)
        x_hi, x_lo = head(xb_ref, h), head(xlo_ref, h)
        pair = mm_tn(y_hi, x_hi) + mm_tn(y_lo, x_hi) + mm_tn(y_hi, x_lo)
        t_ref[h] = pair + pair.T
    for copy in copies:
        copy.wait()


def pair_terms(k, v, x, y, o, mask):
    a = jnp.where(mask, mm_nt(k, x), 0.0).astype(BF16)
    c = jnp.where(mask, mm_nt(v, o) - mm_nt(k, y), 0.0).astype(BF16)
    return mm(c, x) - mm(a, y), mm(a, o)


def own_terms(kv_ref, xb_ref, yo_ref, gk_ref, gv_ref):
    rows, cols = tri(TOK, TOK)
    for h in range(NH):
        gk, gv = pair_terms(
            head(kv_ref, h), head(kv_ref, h, 256), head(xb_ref, h), head(yo_ref, h), head(yo_ref, h, 256), rows <= cols
        )
        gk_ref[:, h * DH : (h + 1) * DH] = gk
        gv_ref[:, h * DH : (h + 1) * DH] = gv


def square():
    r, c = tri(DH, DH)
    return r > c, r == c


def chip_sums(own_ref, other_ref, out_ref):
    below, level = square()
    first, second = own_ref[0] + other_ref[0], own_ref[1] + other_ref[1]
    out_ref[:DH] = jnp.where(below | level, first, second).astype(BF16)
    diagonal = jnp.sum(jnp.where(level, second, 0.0), axis=0, keepdims=True)
    out_ref[DH : DH + 16] = jnp.broadcast_to(diagonal, (16, DH)).astype(BF16)
    for h in range(NH):
        rows = slice(DH + 16 + h * DH, DH + 16 + (h + 1) * DH)
        out_ref[rows] = (own_ref[NH + h] + other_ref[NH + h]).astype(BF16)


def sums_to_send(other_ref, q1_ref, q2_ref, part_ref, both_ref):
    core = lax.rem(lax.axis_index("seq"), 2)
    below, level = square()
    total = q1_ref[...].astype(F32) + q2_ref[...].astype(F32)
    mixed, turned, diagonal = total[:DH], total[:DH].T, total[DH : DH + 1]
    first = jnp.where(below | level, mixed, turned)
    second = jnp.where(level, diagonal, jnp.where(below, turned, mixed))
    crosses = [total[DH + 16 + h * DH : DH + 16 + (h + 1) * DH] for h in range(NH)]
    for at, both in enumerate([first, second] + crosses):
        both_ref[at] = both
        part_ref[at] = both + jnp.where(core == 0, other_ref[at], 0.0)


def early_pairs(lag_ref, xb_ref, yo_ref, early_ref):
    rows, cols = tri(TOK, TOK)
    for h in range(NH):
        gk, gv = pair_terms(
            head(lag_ref, h), head(lag_ref, h, 256), head(xb_ref, h), head(yo_ref, h), head(yo_ref, h, 256), rows > cols
        )
        early_ref[:, h * DH : (h + 1) * DH] = gk.astype(BF16)
        early_ref[:, 256 + h * DH : 256 + (h + 1) * DH] = gv.astype(BF16)


def early_terms(lag_ref, pairs_ref, other_ref, early_ref):
    core = lax.rem(lax.axis_index("seq"), 2)
    for h in range(NH):
        k, v = head(lag_ref, h), head(lag_ref, h, 256)
        sym = jnp.where(core == 1, other_ref[h], 0.0).astype(BF16)
        cross = jnp.where(core == 1, other_ref[NH + h], 0.0).astype(BF16)
        gk = head(pairs_ref, h).astype(F32) - mm(k, sym) + mm_nt(v, cross)
        gv = head(pairs_ref, h, 256).astype(F32) + mm(k, cross)
        early_ref[:, h * DH : (h + 1) * DH] = gk.astype(BF16)
        early_ref[:, 256 + h * DH : 256 + (h + 1) * DH] = gv.astype(BF16)


def base_terms(kv_ref, part_ref, recv_ref, early_ref, gk_in, gv_in, gk_ref, gv_ref):
    for h in range(NH):
        k, v = head(kv_ref, h), head(kv_ref, h, 256)
        s_hi, s_lo = split(part_ref[h] + recv_ref[h])
        c_hi, c_lo = split(part_ref[NH + h] + recv_ref[NH + h])
        cols = slice(h * DH, (h + 1) * DH)
        gk = gk_in[:, cols] + head(early_ref, h).astype(F32) - mm(k, s_hi) - mm(k, s_lo)
        gk_ref[:, cols] = gk + mm_nt(v, c_hi) + mm_nt(v, c_lo)
        gv_ref[:, cols] = gv_in[:, cols] + head(early_ref, h, 256).astype(F32) + mm(k, c_hi) + mm(k, c_lo)


def body(key_rows, values, d_layer, out_weight, saved_solutions, ridge_scale):
    n = lax.axis_size("seq")
    lag = n // 4

    def moved(value, source):
        route = [(source(i), i) for i in range(n) if source(i) is not None and 0 <= source(i) < n]
        return lax.ppermute(value, "seq", route)

    def swapped(value):
        return moved(value, lambda i: i ^ 1)

    st = (2 * NH, DH, DH)
    def around(value, away):
        return lax.ppermute(value, "head", [((i + away) % 8, i) for i in range(8)])

    up, down = around(d_layer, 2), around(d_layer, -2)
    flat = ((TOK, 256), BF16)
    kvd = jnp.concatenate([key_rows, values, d_layer], axis=1)
    own, kv, dv = call(own_states, [(st, F32), ((TOK, 512), BF16), flat], kvd)
    kv_lag = moved(kv, lambda i: i - lag)
    (chip,) = call(chip_states, [((3 * NH, DH, DH), BF16)], own, swapped(own))
    pair = (2, TOK, 256)
    up_two, down_two, across = call(
        to_forward, [(pair, BF16), (pair, BF16), flat], dv, up, down, flops=1 << 34
    )
    up_two, down_two = around(up_two, 1), around(down_two, -1)
    far = [
        (s * 8 + (z + (2 if s % 2 == 0 else -2)) % 8, s * 8 + z) for s in range(n) for z in range(8)
    ]
    across = lax.ppermute(across, ("seq", "head"), far)
    p1 = moved(chip, lambda i: i - 2 if i % 2 == 0 else i - 4)
    p2 = moved(chip, lambda i: i - 6 if i % 2 == 0 else None)
    p1, p2, kv_lag = lax.optimization_barrier((p1, p2, kv_lag))
    part, send, begun, turned, near, xb, xlo, rid = call(
        states_to_send,
        [
            (st, F32), (st, F32), ((TOK, 256), F32), ((4, DH, 256), BF16), ((8, DH, DH), F32), flat, flat,
            ((NH, 8, DH), F32),
        ],
        own, kv_lag, p1, p2, kv, dv, up, down, out_weight, saved_solutions, ridge_scale, size=0, smem=(10,),
    )
    send, across = lax.optimization_barrier((send, across))
    recv = swapped(send)

    y, yo, tl = pl.pallas_call(
        adjoints,
        out_shape=[
            jax.ShapeDtypeStruct((TOK, 256), F32),
            jax.ShapeDtypeStruct((TOK, 512), BF16),
            jax.ShapeDtypeStruct(st, F32),
        ],
        in_specs=[VM] * 14,
        out_specs=[pl.BlockSpec(memory_space=pltpu.HBM), VM, VM],
        scratch_shapes=[pltpu.VMEM((TOK, 256), F32), pltpu.SemaphoreType.DMA((NH,))],
        compiler_params=PARAMS,
        cost_estimate=pl.CostEstimate(flops=1 << 32, bytes_accessed=1 << 19, transcendentals=0),
    )(up_two, down_two, across, out_weight, kv, kv_lag, xb, xlo, part, recv, rid, begun, turned, near)

    (pairs,) = call(early_pairs, [((TOK, 512), BF16)], kv_lag, xb, yo, flops=1 << 26)
    other, pairs = lax.optimization_barrier((swapped(tl), pairs))
    (chip_l,) = call(chip_sums, [((3 * DH + 16, DH), BF16)], tl, other, size=0)
    (early,) = call(early_terms, [((TOK, 512), BF16)], kv_lag, pairs, other, flops=1 << 26)
    early = moved(early, lambda i: i + lag)
    q1 = moved(chip_l, lambda i: i + 2 if i % 2 == 0 else i + 4)
    q2 = moved(chip_l, lambda i: i + 6 if i % 2 == 0 else None)
    gk, gv = call(own_terms, [((TOK, 256), F32)] * 2, kv, xb, yo, flops=1 << 26)
    part_l, both = call(sums_to_send, [(st, F32), (st, F32)], other, q1, q2, size=0)
    recv_l = swapped(both)
    grad_k, grad_v = call(
        base_terms, [((TOK, 256), F32)] * 2, kv, part_l, recv_l, early, gk, gv
    )
    return y, grad_k, grad_v


def solution(mesh):
    return jax.shard_map(
        body,
        mesh=mesh,
        in_specs=(
            P("seq", "head"),
            P("seq", "head"),
            P("seq", "head"),
            P("head", None),
            P("seq", "head"),
            P("head"),
        ),
        out_specs=(P("seq", "head"), P("seq", "head"), P("seq", "head")),
        check_vma=False,
    )
```

```python
import jax
import jax.numpy as jnp
from jax import lax
from jax.experimental import pallas as pl
from jax.experimental.pallas import tpu as pltpu
from jax.sharding import PartitionSpec as P

DH = 128
TOK = 256
NH = 2
ITERS = 8
FINE = 3
EPSILON = 1e-06
F32 = jnp.float32
BF16 = jnp.bfloat16
VM = pl.BlockSpec(memory_space=pltpu.VMEM)
SM = pl.BlockSpec(memory_space=pltpu.SMEM)
PARAMS = pltpu.CompilerParams(vmem_limit_bytes=24 * 1024 * 1024)


def mm(a, b):
    return lax.dot_general(a, b, (((1,), (0,)), ((), ())), preferred_element_type=F32)


def mm_nt(a, b):
    return lax.dot_general(a, b, (((1,), (1,)), ((), ())), preferred_element_type=F32)


def mm_tn(a, b):
    return lax.dot_general(a, b, (((0,), (0,)), ((), ())), preferred_element_type=F32)


def split(a):
    hi = a.astype(BF16)
    return hi, (a - hi.astype(F32)).astype(BF16)


def head(ref, h, base=0):
    return ref[:, base + h * DH : base + (h + 1) * DH]


def tri(rows, cols):
    r = lax.broadcasted_iota(jnp.int32, (rows, cols), 0)
    c = lax.broadcasted_iota(jnp.int32, (rows, cols), 1)
    return r, c


def call(kernel, outs, *args, flops=0, size=1 << 19, smem=()):
    return pl.pallas_call(
        kernel,
        out_shape=[jax.ShapeDtypeStruct(s, d) for s, d in outs],
        in_specs=[SM if i in smem else VM for i in range(len(args))],
        out_specs=[VM] * len(outs),
        compiler_params=PARAMS,
        cost_estimate=pl.CostEstimate(flops=flops, bytes_accessed=size, transcendentals=0),
    )(*args)


def own_states(kvd_ref, t_ref, kv_ref, dv_ref):
    for h in range(NH):
        k = head(kvd_ref, h)
        t_ref[h] = mm_tn(k, k)
        t_ref[NH + h] = mm_tn(head(kvd_ref, h, 256), k)
    kv_ref[...] = kvd_ref[:, :512]
    dv_ref[...] = kvd_ref[:, 512:]


def to_forward(d_ref, up_ref, down_ref, a_ref, b_ref, c_ref):
    core = lax.rem(lax.axis_index("seq"), 2)
    a_ref[0] = d_ref[...]
    a_ref[1] = up_ref[...]
    b_ref[0] = d_ref[...]
    b_ref[1] = down_ref[...]
    c_ref[...] = jnp.where(core == 0, up_ref[...], down_ref[...])


def weight_part(w_ref, away):
    start = pl.multiple_of(lax.rem(lax.axis_index("head") + away, 8) * 256, 256)
    return w_ref[:, pl.ds(start, 256)]


def halves(ref, h, base=0):
    whole = head(ref, h, base)
    return whole[:DH], whole[DH:]


def square():
    r, c = tri(DH, DH)
    return r > c, r == c


def chip_states(own_ref, other_ref, out_ref):
    below, level = square()
    first, second = own_ref[0] + other_ref[0], own_ref[1] + other_ref[1]
    out_ref[:DH] = jnp.where(below | level, first, second).astype(BF16)
    diagonal = jnp.sum(jnp.where(level, second, 0.0), axis=0, keepdims=True)
    out_ref[DH : DH + 16] = jnp.broadcast_to(diagonal, (16, DH)).astype(BF16)
    for h in range(NH):
        hi, lo = split(own_ref[NH + h] + other_ref[NH + h])
        at = DH + 16 + 2 * h * DH
        out_ref[at : at + DH] = hi
        out_ref[at + DH : at + 2 * DH] = lo


def states_to_send(
    t_ref, lag_ref, p1_ref, p2_ref, kv_ref, d_ref, up_ref, down_ref, w_ref, x_ref, ridge_ref,
    part_ref, send_ref, out_ref, turned_ref, near_ref, xb_ref, xlo_ref, rid_ref,
):
    below, level = square()
    total = p1_ref[...].astype(F32) + p2_ref[...].astype(F32)
    mixed, turned = total[:DH], total[:DH].T
    grams = (
        jnp.where(below | level, mixed, turned),
        jnp.where(level, total[DH : DH + 1], jnp.where(below, turned, mixed)),
    )
    core = lax.rem(lax.axis_index("seq"), 2)
    for h in range(NH):
        k = head(lag_ref, h)
        lag_g = mm_tn(k, k)
        lag_s = mm_tn(head(lag_ref, h, NH * DH), k)
        gram = grams[h]
        at = DH + 16 + 2 * h * DH
        state = total[at : at + DH] + total[at + DH : at + 2 * DH]
        for at, lag, part in ((h, lag_g, gram), (NH + h, lag_s, state)):
            part_ref[at] = part
            send_ref[at] = part + jnp.where(core == 0, t_ref[at], lag)
    out = mm_nt(d_ref[...], weight_part(w_ref, 0)) + mm_nt(up_ref[...], weight_part(w_ref, 2))
    out_ref[...] = out + mm_nt(down_ref[...], weight_part(w_ref, 6))
    for h in range(NH):
        keys, lags = halves(kv_ref, h), halves(lag_ref, h)
        for b in range(2):
            turned_ref[2 * h + b, :, :DH] = keys[b].astype(F32).T.astype(BF16)
            turned_ref[2 * h + b, :, DH:] = lags[b].astype(F32).T.astype(BF16)
        near_ref[4 * h] = mm_tn(lags[1], lags[1])
        near_ref[4 * h + 1] = mm_tn(keys[0], keys[0])
        near_ref[4 * h + 2] = mm_tn(halves(lag_ref, h, 256)[1], lags[1])
        near_ref[4 * h + 3] = mm_tn(halves(kv_ref, h, 256)[0], keys[0])
        rid_ref[h] = jnp.full((8, DH), ridge_ref[h], F32)
    xb_ref[...], xlo_ref[...] = split(x_ref[...])


def adjoints(
    a_ref, b_ref, c_ref, w_ref, kv_ref, lag_ref, xb_ref, xlo_ref, part_ref, recv_ref, rid_ref, out_ref, turned_ref,
    near_ref, y_out, yo_ref, t_ref, y_ref, sems,
):
    B = 128
    out = out_ref[...]
    for away, chunk in ((4, c_ref[...]), (1, a_ref[0]), (3, a_ref[1]), (7, b_ref[0]), (5, b_ref[1])):
        out = out + mm_nt(chunk, weight_part(w_ref, away))
    out = out.astype(BF16)
    yo_ref[:, 256:] = out
    rows, cols = tri(B, B)
    low, up = rows >= cols, rows < cols

    rhs, keys, ps, ridges = [], [], [], []
    for h in range(NH):
        k, v = head(kv_ref, h), head(kv_ref, h, 256)
        kl, vl = head(lag_ref, h), head(lag_ref, h, 256)
        gram = part_ref[h] + recv_ref[h]
        state = part_ref[NH + h] + recv_ref[NH + h]
        o = out[:, h * DH : (h + 1) * DH]
        for b in range(2):
            kb, vb = k[b * B : (b + 1) * B], v[b * B : (b + 1) * B]
            klb, vlb = kl[b * B : (b + 1) * B], vl[b * B : (b + 1) * B]
            ob = o[b * B : (b + 1) * B]
            g = gram + near_ref[4 * h + b]
            s = state + near_ref[4 * h + 2 + b]
            g_hi, g_lo = split(g)
            half = jnp.concatenate([g_hi, turned_ref[2 * h + b], g_lo], axis=1)
            rhs.append(jnp.concatenate([half, half], axis=0))
            both = jnp.concatenate([kb, klb], axis=0)
            keys.append(jnp.concatenate([both, both], axis=0))
            sc = jnp.concatenate(
                [jnp.where(low, mm_nt(ob, vb), 0.0), jnp.where(up, mm_nt(ob, vlb), 0.0)], axis=1
            )
            sc_hi, sc_lo = split(sc)
            s_hi, s_lo = split(s)
            p = mm(ob, s_hi) + mm(ob, s_lo)
            p = p + mm(jnp.concatenate([sc_hi, sc_lo], axis=1), keys[-1])
            ps.append(p)
            ridges.append(rid_ref[h, :1])

    for h in range(NH):
        o = out[:, h * DH : (h + 1) * DH]
        t_ref[NH + h] = mm_tn(head(xb_ref, h), o) + mm_tn(head(xlo_ref, h), o)

    n = len(ps)

    def products(vectors, fine):
        firsts = []
        for i in range(n):
            if fine:
                hi, lo = split(vectors[i])
                firsts.append(mm(jnp.concatenate([hi, lo], axis=1), rhs[i]))
            else:
                firsts.append(mm(vectors[i].astype(BF16), rhs[i][:DH, : 3 * B]))
        seconds = []
        for i in range(n):
            r = firsts[i]
            sc = jnp.concatenate(
                [jnp.where(low, r[:, B : 2 * B], 0.0), jnp.where(up, r[:, 2 * B : 3 * B], 0.0)], axis=1
            )
            if fine:
                sc_hi, sc_lo = split(sc)
                seconds.append(mm(jnp.concatenate([sc_hi, sc_lo], axis=1), keys[i]))
            else:
                seconds.append(mm(sc.astype(BF16), keys[i][: 2 * B]))
        images = []
        for i in range(n):
            base = firsts[i][:, :B] + ridges[i] * vectors[i]
            if fine:
                base = base + firsts[i][:, 3 * B :]
            images.append(seconds[i] + base)
        return images

    ys = [jnp.zeros((B, DH), F32)] * n
    rs = list(ps)
    rrs = [jnp.sum(r * r, axis=-1, keepdims=True) for r in rs]
    images = products(ps, True)
    for it in range(ITERS):
        steps = [jnp.sum(ps[i] * images[i], axis=-1, keepdims=True) for i in range(n)]
        alphas = [rrs[i] / (steps[i] + EPSILON) for i in range(n)]
        rs = [rs[i] - alphas[i] * images[i] for i in range(n)]
        ys = [ys[i] + alphas[i] * ps[i] for i in range(n)]
        if it < ITERS - 1:
            fresh = products(rs, it + 1 < FINE)
            nrs = [jnp.sum(r * r, axis=-1, keepdims=True) for r in rs]
            betas = [nrs[i] / (rrs[i] + EPSILON) for i in range(n)]
            ps = [rs[i] + betas[i] * ps[i] for i in range(n)]
            images = [fresh[i] + betas[i] * images[i] for i in range(n)]
            rrs = nrs

    copies = []
    for h in range(NH):
        y = jnp.concatenate([ys[2 * h], ys[2 * h + 1]], axis=0)
        cols = slice(h * DH, (h + 1) * DH)
        y_ref[:, cols] = y
        copies.append(pltpu.make_async_copy(y_ref.at[:, cols], y_out.at[:, cols], sems.at[h]))
        copies[-1].start()
        yo_ref[:, h * DH : (h + 1) * DH] = y.astype(BF16)
        y_hi, y_lo = split(y)
        x_hi, x_lo = head(xb_ref, h), head(xlo_ref, h)
        pair = mm_tn(y_hi, x_hi) + mm_tn(y_lo, x_hi) + mm_tn(y_hi, x_lo)
        t_ref[h] = pair + pair.T
    for copy in copies:
        copy.wait()


def pair_terms(k, v, x, y, o, mask):
    a = jnp.where(mask, mm_nt(k, x), 0.0).astype(BF16)
    c = jnp.where(mask, mm_nt(v, o) - mm_nt(k, y), 0.0).astype(BF16)
    return mm(c, x) - mm(a, y), mm(a, o)


def own_terms(kv_ref, xb_ref, yo_ref, gk_ref, gv_ref):
    rows, cols = tri(TOK, TOK)
    for h in range(NH):
        gk, gv = pair_terms(
            head(kv_ref, h), head(kv_ref, h, 256), head(xb_ref, h), head(yo_ref, h), head(yo_ref, h, 256), rows <= cols
        )
        gk_ref[:, h * DH : (h + 1) * DH] = gk
        gv_ref[:, h * DH : (h + 1) * DH] = gv


def chip_sums(own_ref, other_ref, out_ref):
    below, level = square()
    first, second = own_ref[0] + other_ref[0], own_ref[1] + other_ref[1]
    out_ref[:DH] = jnp.where(below | level, first, second).astype(BF16)
    diagonal = jnp.sum(jnp.where(level, second, 0.0), axis=0, keepdims=True)
    out_ref[DH : DH + 16] = jnp.broadcast_to(diagonal, (16, DH)).astype(BF16)
    for h in range(NH):
        rows = slice(DH + 16 + h * DH, DH + 16 + (h + 1) * DH)
        out_ref[rows] = (own_ref[NH + h] + other_ref[NH + h]).astype(BF16)


def sums_to_send(other_ref, q1_ref, q2_ref, part_ref, both_ref):
    core = lax.rem(lax.axis_index("seq"), 2)
    below, level = square()
    total = q1_ref[...].astype(F32) + q2_ref[...].astype(F32)
    mixed, turned, diagonal = total[:DH], total[:DH].T, total[DH : DH + 1]
    first = jnp.where(below | level, mixed, turned)
    second = jnp.where(level, diagonal, jnp.where(below, turned, mixed))
    crosses = [total[DH + 16 + h * DH : DH + 16 + (h + 1) * DH] for h in range(NH)]
    for at, both in enumerate([first, second] + crosses):
        both_ref[at] = both
        part_ref[at] = both + jnp.where(core == 0, other_ref[at], 0.0)


def early_pairs(lag_ref, xb_ref, yo_ref, early_ref):
    rows, cols = tri(TOK, TOK)
    for h in range(NH):
        gk, gv = pair_terms(
            head(lag_ref, h), head(lag_ref, h, 256), head(xb_ref, h), head(yo_ref, h), head(yo_ref, h, 256), rows > cols
        )
        early_ref[:, h * DH : (h + 1) * DH] = gk.astype(BF16)
        early_ref[:, 256 + h * DH : 256 + (h + 1) * DH] = gv.astype(BF16)


def early_terms(lag_ref, pairs_ref, other_ref, early_ref):
    core = lax.rem(lax.axis_index("seq"), 2)
    for h in range(NH):
        k, v = head(lag_ref, h), head(lag_ref, h, 256)
        sym = jnp.where(core == 1, other_ref[h], 0.0).astype(BF16)
        cross = jnp.where(core == 1, other_ref[NH + h], 0.0).astype(BF16)
        gk = head(pairs_ref, h).astype(F32) - mm(k, sym) + mm_nt(v, cross)
        gv = head(pairs_ref, h, 256).astype(F32) + mm(k, cross)
        early_ref[:, h * DH : (h + 1) * DH] = gk.astype(BF16)
        early_ref[:, 256 + h * DH : 256 + (h + 1) * DH] = gv.astype(BF16)


def base_terms(kv_ref, part_ref, recv_ref, early_ref, gk_in, gv_in, gk_ref, gv_ref):
    for h in range(NH):
        k, v = head(kv_ref, h), head(kv_ref, h, 256)
        s_hi, s_lo = split(part_ref[h] + recv_ref[h])
        c_hi, c_lo = split(part_ref[NH + h] + recv_ref[NH + h])
        cols = slice(h * DH, (h + 1) * DH)
        gk = gk_in[:, cols] + head(early_ref, h).astype(F32) - mm(k, s_hi) - mm(k, s_lo)
        gk_ref[:, cols] = gk + mm_nt(v, c_hi) + mm_nt(v, c_lo)
        gv_ref[:, cols] = gv_in[:, cols] + head(early_ref, h, 256).astype(F32) + mm(k, c_hi) + mm(k, c_lo)


def body(key_rows, values, d_layer, out_weight, saved_solutions, ridge_scale):
    n = lax.axis_size("seq")
    lag = n // 4

    def moved(value, source):
        route = [(source(i), i) for i in range(n) if source(i) is not None and 0 <= source(i) < n]
        return lax.ppermute(value, "seq", route)

    def swapped(value):
        return moved(value, lambda i: i ^ 1)

    st = (2 * NH, DH, DH)
    def around(value, away):
        return lax.ppermute(value, "head", [((i + away) % 8, i) for i in range(8)])

    up, down = around(d_layer, 2), around(d_layer, -2)
    flat = ((TOK, 256), BF16)
    kvd = jnp.concatenate([key_rows, values, d_layer], axis=1)
    own, kv, dv = call(own_states, [(st, F32), ((TOK, 512), BF16), flat], kvd)
    kv_lag = moved(kv, lambda i: i - lag)
    (chip,) = call(chip_states, [((5 * DH + 16, DH), BF16)], own, swapped(own))
    pair = (2, TOK, 256)
    up_two, down_two, across = call(
        to_forward, [(pair, BF16), (pair, BF16), flat], dv, up, down, flops=1 << 34
    )
    up_two, down_two = around(up_two, 1), around(down_two, -1)
    far = [
        (s * 8 + (z + (2 if s % 2 == 0 else -2)) % 8, s * 8 + z) for s in range(n) for z in range(8)
    ]
    across = lax.ppermute(across, ("seq", "head"), far)
    p1 = moved(chip, lambda i: i - 2 if i % 2 == 0 else i - 4)
    p2 = moved(chip, lambda i: i - 6 if i % 2 == 0 else None)
    p1, p2, kv_lag = lax.optimization_barrier((p1, p2, kv_lag))
    part, send, begun, turned, near, xb, xlo, rid = call(
        states_to_send,
        [
            (st, F32), (st, F32), ((TOK, 256), F32), ((4, DH, 256), BF16), ((8, DH, DH), F32), flat, flat,
            ((NH, 8, DH), F32),
        ],
        own, kv_lag, p1, p2, kv, dv, up, down, out_weight, saved_solutions, ridge_scale, size=0, smem=(10,),
    )
    send, across = lax.optimization_barrier((send, across))
    recv = swapped(send)

    y, yo, tl = pl.pallas_call(
        adjoints,
        out_shape=[
            jax.ShapeDtypeStruct((TOK, 256), F32),
            jax.ShapeDtypeStruct((TOK, 512), BF16),
            jax.ShapeDtypeStruct(st, F32),
        ],
        in_specs=[VM] * 14,
        out_specs=[pl.BlockSpec(memory_space=pltpu.HBM), VM, VM],
        scratch_shapes=[pltpu.VMEM((TOK, 256), F32), pltpu.SemaphoreType.DMA((NH,))],
        compiler_params=PARAMS,
        cost_estimate=pl.CostEstimate(flops=1 << 32, bytes_accessed=1 << 19, transcendentals=0),
    )(up_two, down_two, across, out_weight, kv, kv_lag, xb, xlo, part, recv, rid, begun, turned, near)

    (pairs,) = call(early_pairs, [((TOK, 512), BF16)], kv_lag, xb, yo, flops=1 << 26)
    other, pairs = lax.optimization_barrier((swapped(tl), pairs))
    (chip_l,) = call(chip_sums, [((3 * DH + 16, DH), BF16)], tl, other, size=0)
    (early,) = call(early_terms, [((TOK, 512), BF16)], kv_lag, pairs, other, flops=1 << 26)
    early = moved(early, lambda i: i + lag)
    q1 = moved(chip_l, lambda i: i + 2 if i % 2 == 0 else i + 4)
    q2 = moved(chip_l, lambda i: i + 6 if i % 2 == 0 else None)
    gk, gv = call(own_terms, [((TOK, 256), F32)] * 2, kv, xb, yo, flops=1 << 26)
    part_l, both = call(sums_to_send, [(st, F32), (st, F32)], other, q1, q2, size=0)
    recv_l = swapped(both)
    grad_k, grad_v = call(
        base_terms, [((TOK, 256), F32)] * 2, kv, part_l, recv_l, early, gk, gv
    )
    return y, grad_k, grad_v


def solution(mesh):
    return jax.shard_map(
        body,
        mesh=mesh,
        in_specs=(
            P("seq", "head"),
            P("seq", "head"),
            P("seq", "head"),
            P("head", None),
            P("seq", "head"),
            P("head"),
        ),
        out_specs=(P("seq", "head"), P("seq", "head"), P("seq", "head")),
        check_vma=False,
    )
```
